32 devices in a mesh: seq: 16 (over z, x, core), ch: 2 (over y).
Axes of the slice: x: 2, y: 2, z: 4, core: 2. Of those that a mesh axis runs over, the one named last changes fastest.
Arguments:
- query_in: bfloat16 [8192, 2048], P('seq', 'ch'), may hold values from -6 to 6
- key_in: bfloat16 [8192, 2048], P('seq', 'ch'), may hold values from -6 to 6
- value_in: bfloat16 [8192, 2048], P('seq', 'ch'), may hold values from -6 to 6
- filter_taps: float32 [8192, 2048], P('seq', 'ch'), may hold values from -1 to 1
- skip_gain: float32 [2048], P('ch'), may hold values from 0.5 to 1.5
- out_weight: bfloat16 [2048, 2048], P('ch'), may hold values from -0.125 to 0.125
- out_grad: bfloat16 [8192, 2048], P('seq', 'ch'), may hold values from -6 to 6
Outputs:
- mixed_out: bfloat16 [8192, 2048], P('seq', 'ch')
- query_grad: bfloat16 [8192, 2048], P('seq', 'ch')
- key_grad: bfloat16 [8192, 2048], P('seq', 'ch')
- value_grad: bfloat16 [8192, 2048], P('seq', 'ch')
The draws below stay inside these ranges and needn't reach their ends.
All inputs are finite; a program needn't handle non-finite values.
Results may differ from the reference program's by a relative error of at most 0.0049.
Values may be sent and summed in bfloat16 or wider, within the bound.
No kernel may reach another device: no remote copies, remote signals or barrier semaphores. Data moves between devices by JAX's collectives and lax.ppermute only.
A program may use at most 128 MiB of HBM per device.

```python
import math
import jax
import jax.numpy as jnp
from jax import lax

D = 2048
TOKENS = 8192


def draw_filter_taps(key, part):
    key_rate, key_amp = jax.random.split(key, 2)
    positions = jnp.arange(TOKENS, dtype=jnp.float32)[:, None]
    fast_log = math.log(1.0 / 32.0)
    slow_log = math.log(1.0 / TOKENS)
    decay_rates = jnp.exp(jax.random.uniform(key_rate, (D,), dtype=jnp.float32, minval=slow_log, maxval=fast_log))
    amplitude = jnp.clip(jax.random.normal(key_amp, (TOKENS, D), dtype=jnp.float32), -4.0, 4.0)
    norm_scale = jnp.sqrt(2.0 * decay_rates / (1.0 - jnp.exp(-2.0 * decay_rates * TOKENS)))
    return jnp.clip(amplitude * jnp.exp(-decay_rates * positions) * norm_scale, -1.0, 1.0)


def level_of(key, extent, cuts, low, largest):
    def one(axis_at, shards_of):
        heights = jax.random.uniform(jax.random.fold_in(jax.random.fold_in(key, 6), axis_at), (shards_of,), jnp.float32, low / len(cuts), largest / len(cuts))
        return jnp.repeat(jnp.exp(heights), extent[axis_at] // shards_of).reshape((-1,) + (1,) * (len(extent) - axis_at - 1))

    gain = one(*cuts[0])
    for cut in cuts[1:]:
        gain = gain * one(*cut)
    return gain


def bell_draw(own_key, extent, width, most, shards=(), kind=jnp.bfloat16):
    entries = jax.random.normal(own_key, extent, jnp.float32) * width
    if len(shards) > 0:
        entries = level_of(own_key, extent, shards, -0.22, 0.18) * entries
    return jnp.clip(entries, min=-most, max=most).astype(kind)


def setup_inputs(seed: int = 0) -> dict:
    seeds = jax.random.split(jax.random.key(seed), 8)
    return {
        "query_in": bell_draw(seeds[0], (TOKENS, D), 1.0, 6.0, ((0, 16), (1, 2))),
        "key_in": bell_draw(seeds[1], (TOKENS, D), 1.0, 6.0, ((0, 16), (1, 2))),
        "value_in": bell_draw(seeds[2], (TOKENS, D), 1.0, 6.0, ((0, 16), (1, 2))),
        "filter_taps": draw_filter_taps(jax.random.fold_in(seeds[7], 71), 0),
        "skip_gain": jnp.clip(0.5 + 1.0 * jax.random.uniform(seeds[4], (D,), jnp.float32) ** level_of(seeds[4], (D,), ((0, 2),), -0.2, 0.2), 0.5, 1.5),
        "out_weight": bell_draw(seeds[5], (D, D), D ** -0.5, 0.125, ((0, 2),)),
        "out_grad": bell_draw(seeds[6], (TOKENS, D), 1.0, 6.0, ((0, 16), (1, 2))),
    }


def plain_product(taps_spec, signal_spec):
    return taps_spec * signal_spec


def adjoint_product(taps_spec, signal_spec):
    return jnp.conj(taps_spec) * signal_spec


def filter_blocks(signal, taps, combine):
    length, channels = signal.shape
    block_size = math.gcd(channels, 128)
    block_count = channels // block_size
    signal_blocks = signal.reshape(length, block_count, block_size).transpose(1, 0, 2)
    taps_blocks = taps.reshape(length, block_count, block_size).transpose(1, 0, 2)

    def apply_block(operands):
        signal_block, taps_block = operands
        signal_spec = jnp.fft.rfft(signal_block, n=2 * length, axis=0)
        taps_spec = jnp.fft.rfft(taps_block, n=2 * length, axis=0)
        return jnp.fft.irfft(combine(taps_spec, signal_spec), n=2 * length, axis=0)[:length]

    result = lax.map(apply_block, (signal_blocks, taps_blocks))
    return result.transpose(1, 0, 2).reshape(length, channels)


def reference(query_in, key_in, value_in, filter_taps, skip_gain, out_weight, out_grad):
    query_wide = query_in.astype(jnp.float32)
    mixed_in = key_in.astype(jnp.float32) * value_in.astype(jnp.float32)
    conv_out = filter_blocks(mixed_in, filter_taps, plain_product) + skip_gain * mixed_in
    gated_out = (query_wide * conv_out).astype(jnp.bfloat16)
    mixed_out = jnp.dot(gated_out, out_weight, preferred_element_type=jnp.float32).astype(jnp.bfloat16)
    grad_gated = jnp.dot(out_grad, out_weight.T, preferred_element_type=jnp.float32)
    query_grad = (grad_gated * conv_out).astype(jnp.bfloat16)
    grad_conv = grad_gated * query_wide
    grad_mixed = filter_blocks(grad_conv, filter_taps, adjoint_product) + skip_gain * grad_conv
    key_grad = (grad_mixed * value_in.astype(jnp.float32)).astype(jnp.bfloat16)
    value_grad = (grad_mixed * key_in.astype(jnp.float32)).astype(jnp.bfloat16)
    return mixed_out, query_grad, key_grad, value_grad
```

```python
import functools
import math

import jax
import jax.numpy as jnp
import ml_dtypes
import numpy as np
from jax import lax
from jax.experimental import pallas as pl
from jax.experimental.pallas import tpu as pltpu
from jax.sharding import PartitionSpec as P

F32 = jnp.float32
BF16 = jnp.bfloat16
LANES = 128
HALF = 64
FULL_PRECISION = lax.Precision.HIGHEST


def split_high_low(table):
    high = table.astype(ml_dtypes.bfloat16)
    low = (table - high.astype(np.float64)).astype(ml_dtypes.bfloat16)
    return high, low


def slow_positions(devices, tokens_each):
    per_half = tokens_each // 2 // LANES
    half, device, piece = np.meshgrid(
        np.arange(2), np.arange(devices), np.arange(per_half), indexing="ij"
    )
    return (device * 2 * per_half + half * per_half + piece).reshape(-1)


def transform_tables(devices, tokens_each):
    length = devices * tokens_each
    rows = length // LANES
    slow = slow_positions(devices, tokens_each)
    k1 = np.arange(rows)
    n2 = np.arange(LANES)
    turns = (4 * k1[None, :, None] + 1) * (LANES * slow[None, None, :] + n2[:, None, None])
    angle = (turns % (4 * length)) * (2.0 * math.pi / (4 * length))
    cosine, sine = np.cos(angle), np.sin(angle)
    enter = np.concatenate([cosine, -sine], axis=1)
    enter_high, enter_low = split_high_low(enter)
    enter_table = np.concatenate([enter_high, enter_low], axis=2)
    pairs = rows // 2
    leave = np.stack([cosine, -sine], axis=1).reshape(LANES, 2, 2, pairs, rows)
    leave = leave.transpose(0, 4, 2, 1, 3).reshape(LANES, rows, 2 * rows) / length
    leave_high, leave_low = split_high_low(leave)
    leave_table = np.concatenate([leave_high, leave_low], axis=2)
    small = (n2[:, None] * n2[None, :] % LANES) * (2.0 * math.pi / LANES)
    c, s = np.cos(small), np.sin(small)
    forth_high, forth_low = split_high_low(np.block([[c, s], [-s, c]]))
    back_high, back_low = split_high_low(np.block([[c, -s], [s, c]]))
    forth_table = np.concatenate([forth_high, forth_low, forth_high], axis=1)
    back_table = np.concatenate([back_high, back_low, back_high], axis=1)
    return enter_table, forth_table, back_table, leave_table


def low_lanes(rows):
    return lax.broadcasted_iota(jnp.int32, (rows, LANES), 1) < HALF


def swap_lanes(values):
    return pltpu.roll(values, HALF, 1)


def split_float(values):
    high = values.astype(BF16)
    return high, (values - high.astype(F32)).astype(BF16)


def mxu(left, right):
    return jnp.dot(left, right, preferred_element_type=F32)


def convolve_kernel(
    adjoint,
    signal_ref,
    taps_ref,
    enter_ref,
    forth_ref,
    back_ref,
    leave_ref,
    out_ref,
    signal_wide,
    taps_wide,
    entered,
    returned,
    out_wide,
):
    steps = signal_ref.shape[0] // LANES
    rows = 2 * steps
    signal_wide[...] = signal_ref[...].astype(F32)
    taps_wide[...] = taps_ref[...].astype(F32)
    low_steps = low_lanes(steps)

    def enter(n2):
        signal = signal_wide[pl.ds(n2, steps, stride=LANES), :]
        taps = taps_wide[pl.ds(n2, steps, stride=LANES), :]
        first = jnp.where(low_steps, signal, swap_lanes(taps))
        second = jnp.where(low_steps, swap_lanes(signal), taps)
        both = jnp.concatenate([first, second], axis=0).astype(BF16)
        place = pl.multiple_of(n2 * 2 * rows, 2 * rows)
        entered[pl.ds(place, 2 * rows), :] = mxu(
            enter_ref[n2], jnp.concatenate([both, both], axis=0)
        )

    def enter_group(group, _):
        for member in range(4):
            enter(group * 4 + member)
        return 0

    lax.fori_loop(0, LANES // 4, enter_group, 0)
    low = low_lanes(LANES)

    def column(k1):
        real = entered[pl.ds(k1, LANES, stride=2 * rows), :]
        imag = entered[pl.ds(rows + k1, LANES, stride=2 * rows), :]
        return jnp.concatenate([real, imag], axis=0)

    def middle(pair):
        data = jnp.concatenate([column(pair), column(pair + steps)], axis=1)
        high, rest = split_float(data)
        spectrum = mxu(forth_ref[...], jnp.concatenate([high, high, rest], axis=0))
        real_a, real_b = spectrum[:LANES, :LANES], spectrum[:LANES, LANES:]
        imag_a, imag_b = spectrum[LANES:, :LANES], spectrum[LANES:, LANES:]
        signal_real = jnp.where(low, real_a, swap_lanes(real_b))
        signal_imag = jnp.where(low, imag_a, swap_lanes(imag_b))
        taps_real = jnp.where(low, swap_lanes(real_a), real_b)
        taps_imag = jnp.where(low, swap_lanes(imag_a), imag_b)
        if adjoint:
            real = taps_real * signal_real + taps_imag * signal_imag
            imag = taps_real * signal_imag - taps_imag * signal_real
        else:
            real = taps_real * signal_real - taps_imag * signal_imag
            imag = taps_real * signal_imag + taps_imag * signal_real
        high, rest = split_float(jnp.concatenate([real, imag], axis=0))
        place = pl.multiple_of(pair * 2 * LANES, 2 * LANES)
        returned[pl.ds(place, 2 * LANES), :] = mxu(
            back_ref[...], jnp.concatenate([high, high, rest], axis=0)
        )

    def middle_group(group, _):
        for member in range(2):
            middle(group * 2 + member)
        return 0

    lax.fori_loop(0, steps // 2, middle_group, 0)
    low_rows = low_lanes(rows)

    def leave(n2):
        real = returned[pl.ds(n2, steps, stride=2 * LANES), :]
        imag = returned[pl.ds(LANES + n2, steps, stride=2 * LANES), :]
        both = jnp.concatenate([real, imag], axis=0)
        turned = swap_lanes(both)
        data = jnp.concatenate(
            [jnp.where(low_rows, both, turned), jnp.where(low_rows, turned, both)], axis=0
        )
        high, rest = split_float(data)
        table = leave_ref[n2]
        result = mxu(table, jnp.concatenate([high, high], axis=0)) + mxu(
            table[:, : 2 * rows], rest
        )
        out_wide[pl.ds(n2, steps, stride=LANES), :] = jnp.where(
            low_steps, result[:steps], result[steps:]
        )

    def leave_group(group, _):
        for member in range(4):
            leave(group * 4 + member)
        return 0

    lax.fori_loop(0, LANES // 4, leave_group, 0)
    out_ref[...] = out_wide[...].astype(BF16)


def convolve(signal, taps, tables, adjoint):
    devices, places, lanes = signal.shape
    count = devices * places
    rows = 2 * (count // LANES)
    vmem = pl.BlockSpec(memory_space=pltpu.VMEM)
    result = pl.pallas_call(
        functools.partial(convolve_kernel, adjoint),
        out_shape=jax.ShapeDtypeStruct((count, lanes), BF16),
        in_specs=[vmem] * 6,
        out_specs=vmem,
        scratch_shapes=[
            pltpu.VMEM((count, lanes), F32),
            pltpu.VMEM((count, lanes), F32),
            pltpu.VMEM((LANES * 2 * rows, lanes), F32),
            pltpu.VMEM((rows * LANES, lanes), F32),
            pltpu.VMEM((count, lanes), F32),
        ],
        compiler_params=pltpu.CompilerParams(vmem_limit_bytes=56 * 1024 * 1024),
        cost_estimate=pl.CostEstimate(
            flops=6 * 2 * 2 * LANES * 2 * LANES * rows * LANES,
            bytes_accessed=12 * 1024 * 1024,
            transcendentals=0,
        ),
        name="convolve_adjoint" if adjoint else "convolve",
    )(signal.reshape(count, lanes), taps.reshape(count, lanes), *tables)
    return result.reshape(devices, places, lanes)


def pack_block(values):
    places = values.shape[0] // 2
    first, second = values[:places], values[places:]
    low = low_lanes(places)
    return (
        jnp.where(low, first, swap_lanes(second)),
        jnp.where(low, swap_lanes(first), second),
    )


def unpack_block(message_ref):
    first, second = message_ref[0].astype(F32), message_ref[1].astype(F32)
    low = low_lanes(first.shape[0])
    return jnp.concatenate(
        [
            jnp.where(low, first, swap_lanes(second)),
            jnp.where(low, swap_lanes(first), second),
        ],
        axis=0,
    )


def pack_into(message_ref, values):
    first, second = pack_block(values)
    message_ref[0] = first.astype(BF16)
    message_ref[1] = second.astype(BF16)


def mix_kernel(key_ref, value_ref, mixed_ref):
    pack_into(mixed_ref, key_ref[...].astype(F32) * value_ref[...].astype(F32))


def taps_kernel(taps_ref, message_ref):
    pack_into(message_ref, taps_ref[...])


def grad_kernel(gated_ref, query_ref, message_ref):
    pack_into(message_ref, gated_ref[...] * query_ref[...].astype(F32))


def gate_kernel(
    message_ref, key_ref, value_ref, query_ref, skip_ref, grad_ref, gated_ref, query_grad_ref
):
    mixed = key_ref[...].astype(F32) * value_ref[...].astype(F32)
    conv_out = unpack_block(message_ref) + skip_ref[...] * mixed
    gated_ref[...] = (query_ref[...].astype(F32) * conv_out).astype(BF16)
    query_grad_ref[...] = (grad_ref[...] * conv_out).astype(BF16)


def input_grad_kernel(
    message_ref, key_ref, value_ref, query_ref, skip_ref, grad_ref, key_grad_ref, value_grad_ref
):
    grad_conv = grad_ref[...] * query_ref[...].astype(F32)
    grad_mixed = unpack_block(message_ref) + skip_ref[...] * grad_conv
    key_grad_ref[...] = (grad_mixed * value_ref[...].astype(F32)).astype(BF16)
    value_grad_ref[...] = (grad_mixed * key_ref[...].astype(F32)).astype(BF16)


def by_blocks(kernel, shape, inputs, out_kinds):
    tokens, channels = shape
    plain = pl.BlockSpec((tokens, LANES), lambda j: (0, j))
    message = pl.BlockSpec((2, tokens // 2, LANES), lambda j: (j, 0, 0))
    vector = pl.BlockSpec((1, LANES), lambda j: (0, j))

    def spec_of(array):
        if len(array.shape) == 3:
            return message
        return vector if array.shape[0] == 1 else plain

    outs = []
    for kind in out_kinds:
        if kind == "message":
            outs.append(
                jax.ShapeDtypeStruct((2 * channels // LANES, tokens // 2, LANES), BF16)
            )
        else:
            outs.append(jax.ShapeDtypeStruct((tokens, channels), BF16))
    moved = sum(a.size * a.dtype.itemsize for a in list(inputs) + outs)
    return pl.pallas_call(
        kernel,
        grid=(channels // LANES,),
        out_shape=outs,
        in_specs=[spec_of(a) for a in inputs],
        out_specs=[spec_of(a) for a in outs],
        cost_estimate=pl.CostEstimate(
            flops=4 * tokens * channels, bytes_accessed=moved, transcendentals=0
        ),
        compiler_params=pltpu.CompilerParams(vmem_limit_bytes=32 * 1024 * 1024),
    )(*inputs)


def exchange(values):
    return lax.all_to_all(values, "seq", split_axis=0, concat_axis=0, tiled=True)


def swap_pair(values):
    return lax.ppermute(values, "ch", [(0, 1), (1, 0)])


def on_device(query_in, key_in, value_in, filter_taps, skip_gain, out_weight, out_grad):
    devices = lax.axis_size("seq")
    shape = key_in.shape
    tokens, channels = shape
    tables = [jnp.asarray(table) for table in transform_tables(devices, tokens)]
    skip_row = skip_gain.reshape(1, channels)
    mine = lax.axis_index("ch")
    weight_blocks = out_weight.reshape(channels, 2, channels)
    weight_mine = lax.dynamic_index_in_dim(weight_blocks, mine, axis=1, keepdims=False)
    weight_other = lax.dynamic_index_in_dim(weight_blocks, 1 - mine, axis=1, keepdims=False)

    (mixed_sent,) = by_blocks(mix_kernel, shape, [key_in, value_in], ["message"])
    mixed_held = exchange(mixed_sent)
    (taps_sent,) = by_blocks(taps_kernel, shape, [filter_taps], ["message"])
    taps_held = exchange(taps_sent)

    grad_other = swap_pair(out_grad)
    weight_crossed = swap_pair(weight_other)
    over_columns = (((1,), (1,)), ((), ()))
    grad_gated = lax.dot_general(
        out_grad, weight_mine, over_columns, preferred_element_type=F32
    ) + lax.dot_general(grad_other, weight_other, over_columns, preferred_element_type=F32)
    (grad_sent,) = by_blocks(grad_kernel, shape, [grad_gated, query_in], ["message"])
    grad_held = exchange(grad_sent)

    conv_held = convolve(mixed_held, taps_held, tables, False)
    conv_back = exchange(conv_held)
    grad_mixed_held = convolve(grad_held, taps_held, tables, True)
    grad_mixed_back = exchange(grad_mixed_held)

    gated_out, query_grad = by_blocks(
        gate_kernel,
        shape,
        [conv_back, key_in, value_in, query_in, skip_row, grad_gated],
        ["plain", "plain"],
    )
    gated_other = swap_pair(gated_out)
    mixed_out = (
        jnp.dot(gated_out, weight_mine, preferred_element_type=F32)
        + jnp.dot(gated_other, weight_crossed, preferred_element_type=F32)
    ).astype(BF16)
    key_grad, value_grad = by_blocks(
        input_grad_kernel,
        shape,
        [grad_mixed_back, key_in, value_in, query_in, skip_row, grad_gated],
        ["plain", "plain"],
    )
    return (mixed_out, query_grad, key_grad, value_grad)


def phases(row_ids, col_ids, modulus):
    angles = (row_ids[:, None] * col_ids[None, :] % modulus).astype(F32) * (
        2.0 * math.pi / modulus
    )
    return jnp.cos(angles), jnp.sin(angles)


def einsum(form, left, right):
    return jnp.einsum(form, left, right, precision=FULL_PRECISION)


def plain_tables(rows):
    k1 = jnp.arange(rows, dtype=jnp.int32)
    n2 = jnp.arange(LANES, dtype=jnp.int32)
    return (
        phases(4 * k1 + 1, k1, 4 * rows),
        phases(4 * k1 + 1, n2, 4 * rows * LANES),
        phases(n2, n2, LANES),
    )


def plain_spectrum(signal, tables):
    (slow_cos, slow_sin), (turn_cos, turn_sin), (fast_cos, fast_sin) = tables
    real = einsum("kn,njc->kjc", slow_cos, signal)
    imag = -einsum("kn,njc->kjc", slow_sin, signal)
    turn_cos, turn_sin = turn_cos[:, :, None], turn_sin[:, :, None]
    real, imag = real * turn_cos + imag * turn_sin, imag * turn_cos - real * turn_sin
    return (
        einsum("mj,kjc->kmc", fast_cos, real) + einsum("mj,kjc->kmc", fast_sin, imag),
        einsum("mj,kjc->kmc", fast_cos, imag) - einsum("mj,kjc->kmc", fast_sin, real),
    )


def plain_signal(spectrum, tables):
    (slow_cos, slow_sin), (turn_cos, turn_sin), (fast_cos, fast_sin) = tables
    real, imag = spectrum
    real, imag = (
        einsum("jm,kmc->kjc", fast_cos, real) - einsum("jm,kmc->kjc", fast_sin, imag),
        einsum("jm,kmc->kjc", fast_cos, imag) + einsum("jm,kmc->kjc", fast_sin, real),
    )
    turn_cos, turn_sin = turn_cos[:, :, None], turn_sin[:, :, None]
    real, imag = real * turn_cos - imag * turn_sin, imag * turn_cos + real * turn_sin
    result = einsum("kn,kjc->njc", slow_cos, real) - einsum("kn,kjc->njc", slow_sin, imag)
    return result * (1.0 / (slow_cos.shape[0] * LANES))


def on_any_device(query_in, key_in, value_in, filter_taps, skip_gain, out_weight, out_grad):
    tokens, channels = key_in.shape
    rows = lax.axis_size("seq") * tokens // LANES
    tables = plain_tables(rows)

    def to_channels(values):
        held = lax.all_to_all(values, "seq", split_axis=1, concat_axis=0, tiled=True)
        return plain_spectrum(held.reshape(rows, LANES, held.shape[1]), tables)

    def to_tokens(spectrum):
        held = plain_signal(spectrum, tables)
        held = held.reshape(rows * LANES, held.shape[2])
        return lax.all_to_all(held, "seq", split_axis=0, concat_axis=1, tiled=True)

    query = query_in.astype(F32)
    mixed = key_in.astype(F32) * value_in.astype(F32)
    mixed_real, mixed_imag = to_channels(mixed)
    taps_real, taps_imag = to_channels(filter_taps)
    conv_out = skip_gain * mixed + to_tokens(
        (
            mixed_real * taps_real - mixed_imag * taps_imag,
            mixed_real * taps_imag + mixed_imag * taps_real,
        )
    )
    gated_out = (query * conv_out).astype(BF16)
    out_terms = jnp.dot(gated_out, out_weight, preferred_element_type=F32)
    mixed_out = lax.psum_scatter(out_terms, "ch", scatter_dimension=1, tiled=True).astype(BF16)
    grad_gated = lax.dot_general(
        lax.all_gather(out_grad, "ch", axis=1, tiled=True),
        out_weight,
        (((1,), (1,)), ((), ())),
        preferred_element_type=F32,
    )
    query_grad = (grad_gated * conv_out).astype(BF16)
    grad_conv = grad_gated * query
    grad_real, grad_imag = to_channels(grad_conv)
    grad_mixed = skip_gain * grad_conv + to_tokens(
        (
            taps_real * grad_real + taps_imag * grad_imag,
            taps_real * grad_imag - taps_imag * grad_real,
        )
    )
    key_grad = (grad_mixed * value_in.astype(F32)).astype(BF16)
    value_grad = (grad_mixed * key_in.astype(F32)).astype(BF16)
    return (mixed_out, query_grad, key_grad, value_grad)


def solution(mesh):
    spread = P("seq", "ch")
    placed = (spread, spread, spread, spread, P("ch"), P("ch", None), spread)

    def body(*arguments):
        tokens, channels = arguments[1].shape
        fits = (
            lax.axis_size("ch") == 2
            and channels == HALF * lax.axis_size("seq")
            and tokens % (2 * LANES) == 0
        )
        return (on_device if fits else on_any_device)(*arguments)

    return jax.shard_map(
        body, mesh=mesh, in_specs=placed, out_specs=(spread,) * 4, check_vma=False
    )
```

```python
import functools
import math

import jax
import jax.numpy as jnp
import ml_dtypes
import numpy as np
from jax import lax
from jax.experimental import pallas as pl
from jax.experimental.pallas import tpu as pltpu
from jax.sharding import PartitionSpec as P

F32 = jnp.float32
BF16 = jnp.bfloat16
LANES = 128


def split_table(table):
    high = table.astype(ml_dtypes.bfloat16)
    low = (table - high.astype(np.float64)).astype(ml_dtypes.bfloat16)
    return high, low


def transform_tables(devices, tokens_each):
    length = devices * tokens_each
    rows = length // LANES
    pieces = tokens_each // LANES
    row = np.arange(rows)
    n1 = (row % devices) * pieces + row // devices
    k1 = np.arange(rows)
    n2 = np.arange(LANES)

    def waves(turns, modulus):
        angle = (turns % modulus) * (2.0 * math.pi / modulus)
        return np.cos(angle), np.sin(angle)

    c, s = waves((4 * k1 + 1)[:, None] * n1[None, :], 4 * rows)
    high, low = split_table(np.concatenate([c, -s], axis=0))
    enter = np.concatenate([high, low], axis=1)
    high, low = split_table(np.concatenate([c.T, -s.T], axis=1) / length)
    leave = np.concatenate([high, low, high], axis=1)
    c, s = waves(n2[:, None] * n2[None, :], LANES)
    high, low = split_table(np.block([[c, -s], [s, c]]))
    forth = np.concatenate([high, low, high], axis=0)
    high, low = split_table(np.block([[c, s], [-s, c]]))
    back = np.concatenate([high, low, high], axis=0)
    c, s = waves((4 * k1 + 1)[:, None] * n2[None, :], 4 * length)
    turn = np.concatenate([c, s], axis=1).astype(np.float32)
    return enter, turn, np.concatenate([forth, back], axis=0), leave


def split_float(values):
    high = values.astype(BF16)
    return high, (values - high.astype(F32)).astype(BF16)


def mxu(left, right):
    return jnp.dot(left, right, preferred_element_type=F32)


def widen(held_ref, wide):
    for piece in range(wide.shape[0]):
        wide[piece] = held_ref[:, piece * LANES : (piece + 1) * LANES].astype(F32)


def narrow(wide, out_ref):
    for piece in range(wide.shape[0]):
        out_ref[:, piece * LANES : (piece + 1) * LANES] = wide[piece].astype(BF16)


def load_channels(wide, first, stride, devices, group):
    columns = []
    for member in range(group):
        place = pl.ds(first + member, devices, stride=stride)
        columns.append(
            jnp.concatenate([wide[piece, place, :] for piece in range(wide.shape[0])], axis=0)
        )
    return jnp.concatenate(columns, axis=1).astype(BF16)


def to_spectrum(data, group, enter_ref, turn_ref, waves_ref):
    rows = data.shape[0]
    entered = mxu(enter_ref[...], jnp.concatenate([data, data], axis=0))
    cosine, sine = turn_ref[:, :LANES], turn_ref[:, LANES:]
    turned = []
    for member in range(group):
        at = member * LANES
        real, imag = entered[:rows, at : at + LANES], entered[rows:, at : at + LANES]
        turned.append(
            jnp.concatenate([real * cosine + imag * sine, imag * cosine - real * sine], axis=1)
        )
    high, low = split_float(jnp.concatenate(turned, axis=0))
    return mxu(jnp.concatenate([high, high, low], axis=1), waves_ref[: 6 * LANES, :])


def from_spectrum(real, imag, group, turn_ref, waves_ref, leave_ref):
    high, low = split_float(jnp.concatenate([real, imag], axis=1))
    returned = mxu(jnp.concatenate([high, high, low], axis=1), waves_ref[6 * LANES :, :])
    rows = returned.shape[0] // group
    cosine, sine = turn_ref[:, :LANES], turn_ref[:, LANES:]
    turned = []
    for member in range(group):
        at = member * rows
        real, imag = returned[at : at + rows, :LANES], returned[at : at + rows, LANES:]
        turned.append(
            jnp.concatenate([real * cosine - imag * sine, real * sine + imag * cosine], axis=0)
        )
    high, low = split_float(jnp.concatenate(turned, axis=1))
    return mxu(leave_ref[...], jnp.concatenate([high, high, low], axis=0))


def store_channels(wide, first, stride, devices, group, result):
    for member in range(group):
        at = member * LANES
        place = pl.ds(first + member, devices, stride=stride)
        for piece in range(wide.shape[0]):
            row = piece * devices
            wide[piece, place, :] = result[row : row + devices, at : at + LANES]


def forward_kernel(
    devices,
    group,
    held_ref,
    enter_ref,
    turn_ref,
    waves_ref,
    leave_ref,
    out_ref,
    spectrum_ref,
    held_wide,
    out_wide,
):
    step = pl.program_id(0)
    channels = out_ref.shape[0] // devices

    @pl.when(step == 0)
    def _():
        widen(held_ref, held_wide)

    first = step * group
    data = load_channels(held_wide, first, 2 * channels, devices, group)
    taps = load_channels(held_wide, channels + first, 2 * channels, devices, group)
    into = (enter_ref, turn_ref, waves_ref)
    data = to_spectrum(data, group, *into)
    taps = to_spectrum(taps, group, *into)
    spectrum_ref[...] = taps
    data_real, data_imag = data[:, :LANES], data[:, LANES:]
    taps_real, taps_imag = taps[:, :LANES], taps[:, LANES:]
    result = from_spectrum(
        taps_real * data_real - taps_imag * data_imag,
        taps_real * data_imag + taps_imag * data_real,
        group,
        turn_ref,
        waves_ref,
        leave_ref,
    )
    store_channels(out_wide, first, channels, devices, group, result)

    @pl.when(step == pl.num_programs(0) - 1)
    def _():
        narrow(out_wide, out_ref)


def adjoint_kernel(
    devices,
    group,
    held_ref,
    enter_ref,
    turn_ref,
    waves_ref,
    leave_ref,
    spectrum_ref,
    out_ref,
    held_wide,
    out_wide,
):
    step = pl.program_id(0)
    channels = out_ref.shape[0] // devices

    @pl.when(step == 0)
    def _():
        widen(held_ref, held_wide)

    first = step * group
    data = load_channels(held_wide, first, channels, devices, group)
    data = to_spectrum(data, group, enter_ref, turn_ref, waves_ref)
    data_real, data_imag = data[:, :LANES], data[:, LANES:]
    taps_real, taps_imag = spectrum_ref[:, :LANES], spectrum_ref[:, LANES:]
    result = from_spectrum(
        taps_real * data_real + taps_imag * data_imag,
        taps_real * data_imag - taps_imag * data_real,
        group,
        turn_ref,
        waves_ref,
        leave_ref,
    )
    store_channels(out_wide, first, channels, devices, group, result)

    @pl.when(step == pl.num_programs(0) - 1)
    def _():
        narrow(out_wide, out_ref)


GROUP = 16
WIDTH = 512
VMEM_LIMIT = 60 * 1024 * 1024


def whole_block(array):
    return pl.BlockSpec(array.shape, lambda i: (0,) * len(array.shape))


def convolve(held, tables, devices, spectrum=None):
    width, tokens = held.shape
    channels = width // devices // (2 if spectrum is None else 1)
    rows = devices * tokens // LANES
    group = math.gcd(GROUP, channels)
    out = jax.ShapeDtypeStruct((devices * channels, tokens), BF16)
    taps = jax.ShapeDtypeStruct((channels * rows, 2 * LANES), F32)
    taps_block = pl.BlockSpec((group * rows, 2 * LANES), lambda i: (i, 0))
    forward = spectrum is None
    transforms = 3 if forward else 2
    return pl.pallas_call(
        functools.partial(forward_kernel if forward else adjoint_kernel, devices, group),
        grid=(channels // group,),
        out_shape=(out, taps) if forward else out,
        in_specs=[whole_block(held)]
        + [whole_block(table) for table in tables]
        + ([] if forward else [taps_block]),
        out_specs=(whole_block(out), taps_block) if forward else whole_block(out),
        scratch_shapes=[
            pltpu.VMEM((tokens // LANES, width, LANES), F32),
            pltpu.VMEM((tokens // LANES, devices * channels, LANES), F32),
        ],
        compiler_params=pltpu.CompilerParams(vmem_limit_bytes=VMEM_LIMIT),
        cost_estimate=pl.CostEstimate(
            flops=transforms * 8 * 2 * 2 * LANES * 2 * LANES * rows * channels,
            bytes_accessed=8 * 1024 * 1024,
            transcendentals=0,
        ),
        name="convolve" if forward else "correlate",
    )(held, *tables, *([] if forward else [spectrum]))


def rows_of(block, which, channels):
    return block[which * channels : (which + 1) * channels, :]


def mix_kernel(key_ref, value_ref, taps_ref, message_ref):
    targets, both, _ = message_ref.shape
    channels = both // 2
    mixed = (key_ref[...].astype(F32) * value_ref[...].astype(F32)).astype(BF16).T
    taps = taps_ref[...].astype(BF16).T
    for target in range(targets):
        message_ref[target, :channels, :] = rows_of(mixed, target, channels)
        message_ref[target, channels:, :] = rows_of(taps, target, channels)


def grad_kernel(gated_ref, query_ref, message_ref):
    targets, channels, _ = message_ref.shape
    grad = (gated_ref[...] * query_ref[...].astype(F32)).astype(BF16).T
    for target in range(targets):
        message_ref[target] = rows_of(grad, target, channels)


def tokens_first(message_ref):
    targets, channels, tokens = message_ref.shape
    return message_ref[...].reshape(targets * channels, tokens).T.astype(F32)


def gate_kernel(
    message_ref, key_ref, value_ref, query_ref, skip_ref, grad_ref, gated_ref, query_grad_ref
):
    mixed = key_ref[...].astype(F32) * value_ref[...].astype(F32)
    conv_out = tokens_first(message_ref) + skip_ref[...] * mixed
    gated_ref[...] = (query_ref[...].astype(F32) * conv_out).astype(BF16)
    query_grad_ref[...] = (grad_ref[...] * conv_out).astype(BF16)


def input_grad_kernel(
    message_ref, key_ref, value_ref, query_ref, skip_ref, grad_ref, key_grad_ref, value_grad_ref
):
    grad_conv = grad_ref[...] * query_ref[...].astype(F32)
    grad_mixed = tokens_first(message_ref) + skip_ref[...] * grad_conv
    key_grad_ref[...] = (grad_mixed * value_ref[...].astype(F32)).astype(BF16)
    value_grad_ref[...] = (grad_mixed * key_ref[...].astype(F32)).astype(BF16)


def by_blocks(kernel, shape, inputs, outs):
    tokens, channels = shape
    steps = channels // math.gcd(channels, WIDTH)

    def spec_of(array):
        if len(array.shape) == 3:
            targets, rows, _ = array.shape
            return pl.BlockSpec((targets // steps, rows, tokens), lambda j: (j, 0, 0))
        return pl.BlockSpec((array.shape[0], channels // steps), lambda j: (0, j))

    moved = sum(a.size * a.dtype.itemsize for a in list(inputs) + list(outs))
    return pl.pallas_call(
        kernel,
        grid=(steps,),
        out_shape=outs,
        in_specs=[spec_of(a) for a in inputs],
        out_specs=[spec_of(a) for a in outs],
        cost_estimate=pl.CostEstimate(
            flops=4 * tokens * channels, bytes_accessed=moved, transcendentals=0
        ),
        compiler_params=pltpu.CompilerParams(vmem_limit_bytes=VMEM_LIMIT),
    )(*inputs)


def exchange(values):
    return lax.all_to_all(values, "seq", split_axis=0, concat_axis=0, tiled=True)


def swap_pair(values):
    return lax.ppermute(values, "ch", [(0, 1), (1, 0)])


def on_device(query_in, key_in, value_in, filter_taps, skip_gain, out_weight, out_grad):
    devices = lax.axis_size("seq")
    in_pairs = lax.axis_size("ch") == 2
    shape = key_in.shape
    tokens, channels = shape
    each = channels // devices
    tables = [jnp.asarray(table) for table in transform_tables(devices, tokens)]
    skip_row = skip_gain.reshape(1, channels)
    plain = jax.ShapeDtypeStruct(shape, BF16)
    message = jax.ShapeDtypeStruct((devices, each, tokens), BF16)
    double = jax.ShapeDtypeStruct((devices, 2 * each, tokens), BF16)
    over_columns = (((1,), (1,)), ((), ()))

    def project_back(grad, weight):
        return lax.dot_general(grad, weight, over_columns, preferred_element_type=F32)

    if in_pairs:
        grad_other = swap_pair(out_grad)
    (sent,) = by_blocks(mix_kernel, shape, [key_in, value_in, filter_taps], [double])
    held = exchange(sent)

    if in_pairs:
        mine = lax.axis_index("ch") * channels
        other = channels - mine
        weight_mine = lax.dynamic_slice_in_dim(out_weight, mine, channels, axis=1)
        weight_other = lax.dynamic_slice_in_dim(out_weight, other, channels, axis=1)
        grad_other, weight_sent = lax.optimization_barrier((grad_other, weight_other))
        weight_crossed = swap_pair(weight_sent)
        grad_gated = project_back(out_grad, weight_mine) + project_back(grad_other, weight_other)
    else:
        grad_gated = project_back(
            lax.all_gather(out_grad, "ch", axis=1, tiled=True), out_weight
        )
    (grad_sent,) = by_blocks(grad_kernel, shape, [grad_gated, query_in], [message])
    grad_held = exchange(grad_sent)

    conv_held, spectrum = convolve(held.reshape(-1, tokens), tables, devices)
    if in_pairs:
        conv_held, weight_crossed = lax.optimization_barrier((conv_held, weight_crossed))
    conv_back = exchange(conv_held.reshape(message.shape))
    mixed_grad_held = convolve(grad_held.reshape(-1, tokens), tables, devices, spectrum)
    mixed_grad_back = exchange(mixed_grad_held.reshape(message.shape))

    gated_out, query_grad = by_blocks(
        gate_kernel,
        shape,
        [conv_back, key_in, value_in, query_in, skip_row, grad_gated],
        [plain, plain],
    )
    if in_pairs:
        gated_other = swap_pair(gated_out)
        mixed_out = (
            jnp.dot(gated_out, weight_mine, preferred_element_type=F32)
            + jnp.dot(gated_other, weight_crossed, preferred_element_type=F32)
        ).astype(BF16)
    else:
        out_terms = jnp.dot(gated_out, out_weight, preferred_element_type=F32)
        mixed_out = lax.psum_scatter(out_terms, "ch", scatter_dimension=1, tiled=True)
        mixed_out = mixed_out.astype(BF16)
    key_grad, value_grad = by_blocks(
        input_grad_kernel,
        shape,
        [mixed_grad_back, key_in, value_in, query_in, skip_row, grad_gated],
        [plain, plain],
    )
    return (mixed_out, query_grad, key_grad, value_grad)


def solution(mesh):
    spread = P("seq", "ch")
    placed = (spread, spread, spread, spread, P("ch"), P("ch", None), spread)
    return jax.shard_map(
        on_device, mesh=mesh, in_specs=placed, out_specs=(spread,) * 4, check_vma=False
    )
```

```python
import functools
import math

import jax
import jax.numpy as jnp
import ml_dtypes
import numpy as np
from jax import lax
from jax.experimental import pallas as pl
from jax.experimental.pallas import tpu as pltpu
from jax.sharding import PartitionSpec as P

F32 = jnp.float32
BF16 = jnp.bfloat16
LANES = 128


def split_table(table):
    high = table.astype(ml_dtypes.bfloat16)
    low = (table - high.astype(np.float64)).astype(ml_dtypes.bfloat16)
    return high, low


def transform_tables(devices, tokens_each):
    length = devices * tokens_each
    rows = length // LANES
    pieces = tokens_each // LANES
    row = np.arange(rows)
    n1 = (row % devices) * pieces + row // devices
    k1 = np.arange(rows)
    n2 = np.arange(LANES)

    def waves(turns, modulus):
        angle = (turns % modulus) * (2.0 * math.pi / modulus)
        return np.cos(angle), np.sin(angle)

    c, s = waves((4 * k1 + 1)[:, None] * n1[None, :], 4 * rows)
    high, low = split_table(np.concatenate([c, -s], axis=0))
    enter = np.concatenate([high, low], axis=1)
    high, low = split_table(np.concatenate([c.T, -s.T], axis=1) / length)
    leave = np.concatenate([high, low, high], axis=1)
    c, s = waves(n2[:, None] * n2[None, :], LANES)
    high, low = split_table(np.block([[c, -s], [s, c]]))
    forth = np.concatenate([high, low, high], axis=0)
    high, low = split_table(np.block([[c, s], [-s, c]]))
    back = np.concatenate([high, low, high], axis=0)
    c, s = waves((4 * k1 + 1)[:, None] * n2[None, :], 4 * length)
    turn = np.concatenate([c, s], axis=1).astype(np.float32)
    return enter, turn, np.concatenate([forth, back], axis=0), leave


def split_float(values):
    high = values.astype(BF16)
    return high, (values - high.astype(F32)).astype(BF16)


def mxu(left, right):
    return jnp.dot(left, right, preferred_element_type=F32)


def widen(held_ref, wide):
    for piece in range(wide.shape[0]):
        wide[piece] = held_ref[:, piece * LANES : (piece + 1) * LANES].astype(F32)


def narrow(wide, out_ref):
    for piece in range(wide.shape[0]):
        out_ref[:, piece * LANES : (piece + 1) * LANES] = wide[piece].astype(BF16)


def load_channels(wide, first, stride, devices, group):
    columns = []
    for member in range(group):
        place = pl.ds(first + member, devices, stride=stride)
        columns.append(
            jnp.concatenate([wide[piece, place, :] for piece in range(wide.shape[0])], axis=0)
        )
    return jnp.concatenate(columns, axis=1).astype(BF16)


def to_spectrum(data, group, enter_ref, turn_ref, waves_ref):
    rows = data.shape[0]
    entered = mxu(enter_ref[...], jnp.concatenate([data, data], axis=0))
    cosine, sine = turn_ref[:, :LANES], turn_ref[:, LANES:]
    turned = []
    for member in range(group):
        at = member * LANES
        real, imag = entered[:rows, at : at + LANES], entered[rows:, at : at + LANES]
        turned.append(
            jnp.concatenate([real * cosine + imag * sine, imag * cosine - real * sine], axis=1)
        )
    high, low = split_float(jnp.concatenate(turned, axis=0))
    return mxu(jnp.concatenate([high, high, low], axis=1), waves_ref[: 6 * LANES, :])


def from_spectrum(real, imag, group, turn_ref, waves_ref, leave_ref):
    high, low = split_float(jnp.concatenate([real, imag], axis=1))
    returned = mxu(jnp.concatenate([high, high, low], axis=1), waves_ref[6 * LANES :, :])
    rows = returned.shape[0] // group
    cosine, sine = turn_ref[:, :LANES], turn_ref[:, LANES:]
    turned = []
    for member in range(group):
        at = member * rows
        real, imag = returned[at : at + rows, :LANES], returned[at : at + rows, LANES:]
        turned.append(
            jnp.concatenate([real * cosine - imag * sine, real * sine + imag * cosine], axis=0)
        )
    high, low = split_float(jnp.concatenate(turned, axis=1))
    return mxu(leave_ref[...], jnp.concatenate([high, high, low], axis=0))


def store_channels(wide, first, stride, devices, group, result):
    for member in range(group):
        at = member * LANES
        place = pl.ds(first + member, devices, stride=stride)
        for piece in range(wide.shape[0]):
            row = piece * devices
            wide[piece, place, :] = result[row : row + devices, at : at + LANES]


def forward_kernel(
    devices,
    group,
    held_ref,
    enter_ref,
    turn_ref,
    waves_ref,
    leave_ref,
    out_ref,
    spectrum_ref,
    held_wide,
    out_wide,
):
    step = pl.program_id(0)
    channels = out_ref.shape[0] // devices

    @pl.when(step == 0)
    def _():
        widen(held_ref, held_wide)

    first = step * group
    data = load_channels(held_wide, first, 2 * channels, devices, group)
    taps = load_channels(held_wide, channels + first, 2 * channels, devices, group)
    into = (enter_ref, turn_ref, waves_ref)
    data = to_spectrum(data, group, *into)
    taps = to_spectrum(taps, group, *into)
    spectrum_ref[...] = taps
    data_real, data_imag = data[:, :LANES], data[:, LANES:]
    taps_real, taps_imag = taps[:, :LANES], taps[:, LANES:]
    result = from_spectrum(
        taps_real * data_real - taps_imag * data_imag,
        taps_real * data_imag + taps_imag * data_real,
        group,
        turn_ref,
        waves_ref,
        leave_ref,
    )
    store_channels(out_wide, first, channels, devices, group, result)

    @pl.when(step == pl.num_programs(0) - 1)
    def _():
        narrow(out_wide, out_ref)


def adjoint_kernel(
    devices,
    group,
    held_ref,
    enter_ref,
    turn_ref,
    waves_ref,
    leave_ref,
    spectrum_ref,
    out_ref,
    held_wide,
    out_wide,
):
    step = pl.program_id(0)
    channels = out_ref.shape[0] // devices

    @pl.when(step == 0)
    def _():
        widen(held_ref, held_wide)

    first = step * group
    data = load_channels(held_wide, first, channels, devices, group)
    data = to_spectrum(data, group, enter_ref, turn_ref, waves_ref)
    data_real, data_imag = data[:, :LANES], data[:, LANES:]
    taps_real, taps_imag = spectrum_ref[:, :LANES], spectrum_ref[:, LANES:]
    result = from_spectrum(
        taps_real * data_real + taps_imag * data_imag,
        taps_real * data_imag - taps_imag * data_real,
        group,
        turn_ref,
        waves_ref,
        leave_ref,
    )
    store_channels(out_wide, first, channels, devices, group, result)

    @pl.when(step == pl.num_programs(0) - 1)
    def _():
        narrow(out_wide, out_ref)


GROUP = 16
WIDTH = 512
VMEM_LIMIT = 60 * 1024 * 1024


def whole_block(array):
    return pl.BlockSpec(array.shape, lambda i: (0,) * len(array.shape))


def convolve(held, tables, devices, spectrum=None):
    width, tokens = held.shape
    channels = width // devices // (2 if spectrum is None else 1)
    rows = devices * tokens // LANES
    group = math.gcd(GROUP, channels)
    out = jax.ShapeDtypeStruct((devices * channels, tokens), BF16)
    taps = jax.ShapeDtypeStruct((channels * rows, 2 * LANES), F32)
    taps_block = pl.BlockSpec((group * rows, 2 * LANES), lambda i: (i, 0))
    forward = spectrum is None
    transforms = 3 if forward else 2
    return pl.pallas_call(
        functools.partial(forward_kernel if forward else adjoint_kernel, devices, group),
        grid=(channels // group,),
        out_shape=(out, taps) if forward else out,
        in_specs=[whole_block(held)]
        + [whole_block(table) for table in tables]
        + ([] if forward else [taps_block]),
        out_specs=(whole_block(out), taps_block) if forward else whole_block(out),
        scratch_shapes=[
            pltpu.VMEM((tokens // LANES, width, LANES), F32),
            pltpu.VMEM((tokens // LANES, devices * channels, LANES), F32),
        ],
        compiler_params=pltpu.CompilerParams(vmem_limit_bytes=VMEM_LIMIT),
        cost_estimate=pl.CostEstimate(
            flops=transforms * 8 * 2 * 2 * LANES * 2 * LANES * rows * channels,
            bytes_accessed=8 * 1024 * 1024,
            transcendentals=0,
        ),
        name="convolve" if forward else "correlate",
    )(held, *tables, *([] if forward else [spectrum]))


def rows_of(block, which, channels):
    return block[which * channels : (which + 1) * channels, :]


def mix_kernel(key_ref, value_ref, taps_ref, message_ref):
    targets, both, _ = message_ref.shape
    channels = both // 2
    mixed = (key_ref[...].astype(F32) * value_ref[...].astype(F32)).astype(BF16).T
    taps = taps_ref[...].astype(BF16).T
    for target in range(targets):
        message_ref[target, :channels, :] = rows_of(mixed, target, channels)
        message_ref[target, channels:, :] = rows_of(taps, target, channels)


def grad_kernel(gated_ref, query_ref, message_ref):
    targets, channels, _ = message_ref.shape
    grad = (gated_ref[...] * query_ref[...].astype(F32)).astype(BF16).T
    for target in range(targets):
        message_ref[target] = rows_of(grad, target, channels)


def tokens_first(message_ref):
    targets, channels, tokens = message_ref.shape
    return message_ref[...].reshape(targets * channels, tokens).T.astype(F32)


def gate_kernel(message_ref, key_ref, value_ref, query_ref, skip_ref, gated_ref):
    mixed = key_ref[...].astype(F32) * value_ref[...].astype(F32)
    conv_out = tokens_first(message_ref) + skip_ref[...] * mixed
    gated_ref[...] = (query_ref[...].astype(F32) * conv_out).astype(BF16)


def query_grad_kernel(message_ref, key_ref, value_ref, skip_ref, grad_ref, query_grad_ref):
    mixed = key_ref[...].astype(F32) * value_ref[...].astype(F32)
    conv_out = tokens_first(message_ref) + skip_ref[...] * mixed
    query_grad_ref[...] = (grad_ref[...] * conv_out).astype(BF16)


def input_grad_kernel(
    message_ref, key_ref, value_ref, query_ref, skip_ref, grad_ref, key_grad_ref, value_grad_ref
):
    grad_conv = grad_ref[...] * query_ref[...].astype(F32)
    grad_mixed = tokens_first(message_ref) + skip_ref[...] * grad_conv
    key_grad_ref[...] = (grad_mixed * value_ref[...].astype(F32)).astype(BF16)
    value_grad_ref[...] = (grad_mixed * key_ref[...].astype(F32)).astype(BF16)


def by_blocks(kernel, shape, inputs, outs):
    tokens, channels = shape
    steps = channels // math.gcd(channels, WIDTH)

    def spec_of(array):
        if len(array.shape) == 3:
            targets, rows, _ = array.shape
            return pl.BlockSpec((targets // steps, rows, tokens), lambda j: (j, 0, 0))
        return pl.BlockSpec((array.shape[0], channels // steps), lambda j: (0, j))

    moved = sum(a.size * a.dtype.itemsize for a in list(inputs) + list(outs))
    return pl.pallas_call(
        kernel,
        grid=(steps,),
        out_shape=outs,
        in_specs=[spec_of(a) for a in inputs],
        out_specs=[spec_of(a) for a in outs],
        cost_estimate=pl.CostEstimate(
            flops=4 * tokens * channels, bytes_accessed=moved, transcendentals=0
        ),
        compiler_params=pltpu.CompilerParams(vmem_limit_bytes=VMEM_LIMIT),
    )(*inputs)


def exchange(values):
    return lax.all_to_all(values, "seq", split_axis=0, concat_axis=0, tiled=True)


def swap_pair(values):
    return lax.ppermute(values, "ch", [(0, 1), (1, 0)])


def on_device(query_in, key_in, value_in, filter_taps, skip_gain, out_weight, out_grad):
    devices = lax.axis_size("seq")
    in_pairs = lax.axis_size("ch") == 2
    shape = key_in.shape
    tokens, channels = shape
    each = channels // devices
    tables = [jnp.asarray(table) for table in transform_tables(devices, tokens)]
    skip_row = skip_gain.reshape(1, channels)
    plain = jax.ShapeDtypeStruct(shape, BF16)
    message = jax.ShapeDtypeStruct((devices, each, tokens), BF16)
    double = jax.ShapeDtypeStruct((devices, 2 * each, tokens), BF16)
    over_columns = (((1,), (1,)), ((), ()))

    def project_back(grad, weight):
        return lax.dot_general(grad, weight, over_columns, preferred_element_type=F32)

    if in_pairs:
        grad_other = swap_pair(out_grad)
    (sent,) = by_blocks(mix_kernel, shape, [key_in, value_in, filter_taps], [double])
    held = exchange(sent)

    if in_pairs:
        mine = lax.axis_index("ch") * channels
        other = channels - mine
        weight_mine = lax.dynamic_slice_in_dim(out_weight, mine, channels, axis=1)
        weight_other = lax.dynamic_slice_in_dim(out_weight, other, channels, axis=1)
        grad_other, weight_sent = lax.optimization_barrier((grad_other, weight_other))
        weight_crossed = swap_pair(weight_sent)
        grad_gated = project_back(out_grad, weight_mine) + project_back(grad_other, weight_other)
    else:
        grad_gated = project_back(
            lax.all_gather(out_grad, "ch", axis=1, tiled=True), out_weight
        )
    (grad_sent,) = by_blocks(grad_kernel, shape, [grad_gated, query_in], [message])
    grad_held = exchange(grad_sent)

    conv_held, spectrum = convolve(held.reshape(-1, tokens), tables, devices)
    if in_pairs:
        conv_held, weight_crossed = lax.optimization_barrier((conv_held, weight_crossed))
    conv_back = exchange(conv_held.reshape(message.shape))
    mixed_grad_held = convolve(grad_held.reshape(-1, tokens), tables, devices, spectrum)
    (gated_out,) = by_blocks(
        gate_kernel, shape, [conv_back, key_in, value_in, query_in, skip_row], [plain]
    )
    mixed_grad_back = exchange(mixed_grad_held.reshape(message.shape))
    (query_grad,) = by_blocks(
        query_grad_kernel, shape, [conv_back, key_in, value_in, skip_row, grad_gated], [plain]
    )
    own_terms = jnp.dot(
        gated_out, weight_mine if in_pairs else out_weight, preferred_element_type=F32
    )
    if in_pairs:
        gated_other = swap_pair(gated_out)
        own_terms, query_grad, mixed_grad_back = lax.optimization_barrier(
            (own_terms, query_grad, mixed_grad_back)
        )
        mixed_out = own_terms + jnp.dot(
            gated_other, weight_crossed, preferred_element_type=F32
        )
    else:
        mixed_out = lax.psum_scatter(own_terms, "ch", scatter_dimension=1, tiled=True)
    key_grad, value_grad = by_blocks(
        input_grad_kernel,
        shape,
        [mixed_grad_back, key_in, value_in, query_in, skip_row, grad_gated],
        [plain, plain],
    )
    return (mixed_out.astype(BF16), query_grad, key_grad, value_grad)


def solution(mesh):
    spread = P("seq", "ch")
    placed = (spread, spread, spread, spread, P("ch"), P("ch", None), spread)
    return jax.shard_map(
        on_device, mesh=mesh, in_specs=placed, out_specs=(spread,) * 4, check_vma=False
    )
```

```python
import functools
import math

import jax
import jax.numpy as jnp
import ml_dtypes
import numpy as np
from jax import lax
from jax.experimental import pallas as pl
from jax.experimental.pallas import tpu as pltpu
from jax.sharding import PartitionSpec as P

F32 = jnp.float32
BF16 = jnp.bfloat16
LANES = 128


def split_table(table):
    high = table.astype(ml_dtypes.bfloat16)
    low = (table - high.astype(np.float64)).astype(ml_dtypes.bfloat16)
    return high, low


def transform_tables(devices, tokens_each):
    length = devices * tokens_each
    rows = length // LANES
    pieces = tokens_each // LANES
    row = np.arange(rows)
    n1 = (row % devices) * pieces + row // devices
    k1 = np.arange(rows)
    n2 = np.arange(LANES)

    def waves(turns, modulus):
        angle = (turns % modulus) * (2.0 * math.pi / modulus)
        return np.cos(angle), np.sin(angle)

    c, s = waves((4 * k1 + 1)[:, None] * n1[None, :], 4 * rows)
    high, low = split_table(np.concatenate([c, -s], axis=0))
    enter = np.concatenate([high, low], axis=1)
    high, low = split_table(np.concatenate([c.T, -s.T], axis=1) / length)
    leave = np.concatenate([high, low, high], axis=1)
    c, s = waves(n2[:, None] * n2[None, :], LANES)
    high, low = split_table(np.block([[c, -s], [s, c]]))
    forth = np.concatenate([high, low, high], axis=0)
    high, low = split_table(np.block([[c, s], [-s, c]]))
    back = np.concatenate([high, low, high], axis=0)
    c, s = waves((4 * k1 + 1)[:, None] * n2[None, :], 4 * length)
    turn = np.concatenate([c, s], axis=1).astype(np.float32)
    return enter, turn, np.concatenate([forth, back], axis=0), leave


def split_float(values):
    high = values.astype(BF16)
    return high, (values - high.astype(F32)).astype(BF16)


def mxu(left, right):
    return jnp.dot(left, right, preferred_element_type=F32)


def widen(held_ref, wide):
    for piece in range(wide.shape[0]):
        wide[piece] = held_ref[:, piece * LANES : (piece + 1) * LANES].astype(F32)


def narrow(wide, out_ref):
    for piece in range(wide.shape[0]):
        out_ref[:, piece * LANES : (piece + 1) * LANES] = wide[piece].astype(BF16)


def load_channels(wide, first, stride, devices, group):
    columns = []
    for member in range(group):
        place = pl.ds(first + member, devices, stride=stride)
        columns.append(
            jnp.concatenate([wide[piece, place, :] for piece in range(wide.shape[0])], axis=0)
        )
    return jnp.concatenate(columns, axis=1).astype(BF16)


def to_spectrum(data, group, enter_ref, turn_ref, waves_ref):
    rows = data.shape[0]
    entered = mxu(enter_ref[...], jnp.concatenate([data, data], axis=0))
    cosine, sine = turn_ref[:, :LANES], turn_ref[:, LANES:]
    turned = []
    for member in range(group):
        at = member * LANES
        real, imag = entered[:rows, at : at + LANES], entered[rows:, at : at + LANES]
        turned.append(
            jnp.concatenate([real * cosine + imag * sine, imag * cosine - real * sine], axis=1)
        )
    high, low = split_float(jnp.concatenate(turned, axis=0))
    return mxu(jnp.concatenate([high, high, low], axis=1), waves_ref[: 6 * LANES, :])


def from_spectrum(real, imag, group, turn_ref, waves_ref, leave_ref):
    high, low = split_float(jnp.concatenate([real, imag], axis=1))
    returned = mxu(jnp.concatenate([high, high, low], axis=1), waves_ref[6 * LANES :, :])
    rows = returned.shape[0] // group
    cosine, sine = turn_ref[:, :LANES], turn_ref[:, LANES:]
    turned = []
    for member in range(group):
        at = member * rows
        real, imag = returned[at : at + rows, :LANES], returned[at : at + rows, LANES:]
        turned.append(
            jnp.concatenate([real * cosine - imag * sine, real * sine + imag * cosine], axis=0)
        )
    high, low = split_float(jnp.concatenate(turned, axis=1))
    return mxu(leave_ref[...], jnp.concatenate([high, high, low], axis=0))


def store_channels(wide, first, stride, devices, group, result):
    for member in range(group):
        at = member * LANES
        place = pl.ds(first + member, devices, stride=stride)
        for piece in range(wide.shape[0]):
            row = piece * devices
            wide[piece, place, :] = result[row : row + devices, at : at + LANES]


def forward_kernel(
    devices,
    group,
    held_ref,
    enter_ref,
    turn_ref,
    waves_ref,
    leave_ref,
    out_ref,
    spectrum_ref,
    held_wide,
    out_wide,
):
    step = pl.program_id(0)
    channels = out_ref.shape[0] // devices

    @pl.when(step == 0)
    def _():
        widen(held_ref, held_wide)

    first = step * group
    data = load_channels(held_wide, first, 2 * channels, devices, group)
    taps = load_channels(held_wide, channels + first, 2 * channels, devices, group)
    into = (enter_ref, turn_ref, waves_ref)
    data = to_spectrum(data, group, *into)
    taps = to_spectrum(taps, group, *into)
    spectrum_ref[...] = taps
    data_real, data_imag = data[:, :LANES], data[:, LANES:]
    taps_real, taps_imag = taps[:, :LANES], taps[:, LANES:]
    result = from_spectrum(
        taps_real * data_real - taps_imag * data_imag,
        taps_real * data_imag + taps_imag * data_real,
        group,
        turn_ref,
        waves_ref,
        leave_ref,
    )
    store_channels(out_wide, first, channels, devices, group, result)

    @pl.when(step == pl.num_programs(0) - 1)
    def _():
        narrow(out_wide, out_ref)


def adjoint_kernel(
    devices,
    group,
    held_ref,
    enter_ref,
    turn_ref,
    waves_ref,
    leave_ref,
    spectrum_ref,
    out_ref,
    held_wide,
    out_wide,
):
    step = pl.program_id(0)
    channels = out_ref.shape[0] // devices

    @pl.when(step == 0)
    def _():
        widen(held_ref, held_wide)

    first = step * group
    data = load_channels(held_wide, first, channels, devices, group)
    data = to_spectrum(data, group, enter_ref, turn_ref, waves_ref)
    data_real, data_imag = data[:, :LANES], data[:, LANES:]
    taps_real, taps_imag = spectrum_ref[:, :LANES], spectrum_ref[:, LANES:]
    result = from_spectrum(
        taps_real * data_real + taps_imag * data_imag,
        taps_real * data_imag - taps_imag * data_real,
        group,
        turn_ref,
        waves_ref,
        leave_ref,
    )
    store_channels(out_wide, first, channels, devices, group, result)

    @pl.when(step == pl.num_programs(0) - 1)
    def _():
        narrow(out_wide, out_ref)


GROUP = 16
WIDTH = 512
VMEM_LIMIT = 60 * 1024 * 1024
LAST_LIMIT = 48 * 1024 * 1024


def whole_block(array):
    return pl.BlockSpec(array.shape, lambda i: (0,) * len(array.shape))


def convolve(held, tables, devices, spectrum=None):
    width, tokens = held.shape
    channels = width // devices // (2 if spectrum is None else 1)
    rows = devices * tokens // LANES
    group = math.gcd(GROUP, channels)
    out = jax.ShapeDtypeStruct((devices * channels, tokens), BF16)
    taps = jax.ShapeDtypeStruct((channels * rows, 2 * LANES), F32)
    taps_block = pl.BlockSpec((group * rows, 2 * LANES), lambda i: (i, 0))
    forward = spectrum is None
    transforms = 3 if forward else 2
    return pl.pallas_call(
        functools.partial(forward_kernel if forward else adjoint_kernel, devices, group),
        grid=(channels // group,),
        out_shape=(out, taps) if forward else out,
        in_specs=[whole_block(held)]
        + [whole_block(table) for table in tables]
        + ([] if forward else [taps_block]),
        out_specs=(whole_block(out), taps_block) if forward else whole_block(out),
        scratch_shapes=[
            pltpu.VMEM((tokens // LANES, width, LANES), F32),
            pltpu.VMEM((tokens // LANES, devices * channels, LANES), F32),
        ],
        compiler_params=pltpu.CompilerParams(vmem_limit_bytes=VMEM_LIMIT),
        cost_estimate=pl.CostEstimate(
            flops=transforms * 8 * 2 * 2 * LANES * 2 * LANES * rows * channels,
            bytes_accessed=8 * 1024 * 1024,
            transcendentals=0,
        ),
        name="convolve" if forward else "correlate",
    )(held, *tables, *([] if forward else [spectrum]))


def rows_of(block, which, channels):
    return block[which * channels : (which + 1) * channels, :]


def mix_kernel(key_ref, value_ref, taps_ref, message_ref):
    targets, both, _ = message_ref.shape
    channels = both // 2
    mixed = (key_ref[...].astype(F32) * value_ref[...].astype(F32)).astype(BF16).T
    taps = taps_ref[...].astype(BF16).T
    for target in range(targets):
        message_ref[target, :channels, :] = rows_of(mixed, target, channels)
        message_ref[target, channels:, :] = rows_of(taps, target, channels)


def grad_kernel(gated_ref, query_ref, message_ref):
    targets, channels, _ = message_ref.shape
    grad = (gated_ref[...] * query_ref[...].astype(F32)).astype(BF16).T
    for target in range(targets):
        message_ref[target] = rows_of(grad, target, channels)


def tokens_first(message_ref):
    targets, channels, tokens = message_ref.shape
    return message_ref[...].reshape(targets * channels, tokens).T.astype(F32)


def gate_kernel(message_ref, key_ref, value_ref, query_ref, skip_ref, gated_ref):
    mixed = key_ref[...].astype(F32) * value_ref[...].astype(F32)
    conv_out = tokens_first(message_ref) + skip_ref[...] * mixed
    gated_ref[...] = (query_ref[...].astype(F32) * conv_out).astype(BF16)


def query_grad_kernel(
    message_ref, key_ref, value_ref, query_ref, skip_ref, grad_ref, query_grad_ref, near_ref
):
    width = key_ref.shape[1]
    for at, ref in enumerate((key_ref, value_ref, query_ref)):
        near_ref[:, at * width : (at + 1) * width] = ref[...]
    mixed = key_ref[...].astype(F32) * value_ref[...].astype(F32)
    conv_out = tokens_first(message_ref) + skip_ref[...] * mixed
    query_grad_ref[...] = (grad_ref[...] * conv_out).astype(BF16)


def input_grad_kernel(
    message_ref, near_ref, skip_ref, grad_ref, key_grad_ref, value_grad_ref
):
    width = grad_ref.shape[1]
    key, value, query = (
        near_ref[:, at * width : (at + 1) * width].astype(F32) for at in range(3)
    )
    grad_mixed = tokens_first(message_ref) + skip_ref[...] * (grad_ref[...] * query)
    key_grad_ref[...] = (grad_mixed * value).astype(BF16)
    value_grad_ref[...] = (grad_mixed * key).astype(BF16)


def project_kernel(terms_ref, gated_ref, weight_ref, out_ref):
    total = terms_ref[...] + mxu(gated_ref[...], weight_ref[...])
    out_ref[...] = total.astype(out_ref.dtype)


def project(terms, gated, weight, at, kind):
    tokens, depth = gated.shape
    width = math.gcd(terms.shape[1], WIDTH)
    block = pl.BlockSpec((tokens, width), lambda j: (0, j))
    return pl.pallas_call(
        project_kernel,
        grid=(terms.shape[1] // width,),
        out_shape=jax.ShapeDtypeStruct(terms.shape, kind),
        in_specs=[
            block,
            pl.BlockSpec((tokens, depth), lambda j: (0, 0)),
            pl.BlockSpec((depth, width), lambda j: (at, j)),
        ],
        out_specs=block,
        cost_estimate=pl.CostEstimate(
            flops=2 * tokens * depth * terms.shape[1],
            bytes_accessed=6 * terms.size,
            transcendentals=0,
        ),
        compiler_params=pltpu.CompilerParams(vmem_limit_bytes=VMEM_LIMIT),
        name="project",
    )(terms, gated, weight)


def by_blocks(kernel, shape, inputs, outs, only=None, vmem_limit=None):
    tokens, channels = shape
    steps = channels // math.gcd(channels, WIDTH)
    width = channels // steps

    def spec_of(array):
        def at(j):
            return j if only is None or array.shape[-1] == width else only

        if len(array.shape) == 3:
            targets, rows, _ = array.shape
            return pl.BlockSpec(
                (targets // steps, rows, tokens), lambda j: (j if only is None else only, 0, 0)
            )
        size = width if only is not None else array.shape[1] // steps
        return pl.BlockSpec((array.shape[0], size), lambda j: (0, at(j)))

    moved = sum(a.size * a.dtype.itemsize for a in list(inputs) + list(outs))
    return pl.pallas_call(
        kernel,
        grid=(steps if only is None else 1,),
        out_shape=outs,
        in_specs=[spec_of(a) for a in inputs],
        out_specs=[spec_of(a) for a in outs],
        cost_estimate=pl.CostEstimate(
            flops=4 * tokens * channels, bytes_accessed=moved, transcendentals=0
        ),
        compiler_params=pltpu.CompilerParams(vmem_limit_bytes=vmem_limit or VMEM_LIMIT),
    )(*inputs)


def exchange(values):
    return lax.all_to_all(values, "seq", split_axis=0, concat_axis=0, tiled=True)


def swap_pair(values):
    return lax.ppermute(values, "ch", [(0, 1), (1, 0)])


def on_device(query_in, key_in, value_in, filter_taps, skip_gain, out_weight, out_grad):
    devices = lax.axis_size("seq")
    in_pairs = lax.axis_size("ch") == 2
    shape = key_in.shape
    tokens, channels = shape
    each = channels // devices
    tables = [jnp.asarray(table) for table in transform_tables(devices, tokens)]
    skip_row = skip_gain.reshape(1, channels)
    plain = jax.ShapeDtypeStruct(shape, BF16)
    message = jax.ShapeDtypeStruct((devices, each, tokens), BF16)
    double = jax.ShapeDtypeStruct((devices, 2 * each, tokens), BF16)
    over_columns = (((1,), (1,)), ((), ()))

    def project_back(grad, weight):
        return lax.dot_general(grad, weight, over_columns, preferred_element_type=F32)

    if in_pairs:
        grad_other = swap_pair(out_grad)
    (sent,) = by_blocks(mix_kernel, shape, [key_in, value_in, filter_taps], [double])
    held = exchange(sent)

    if in_pairs:
        mine = lax.axis_index("ch") * channels
        other = channels - mine
        weight_mine = lax.dynamic_slice_in_dim(out_weight, mine, channels, axis=1)
        weight_other = lax.dynamic_slice_in_dim(out_weight, other, channels, axis=1)
        grad_other, weight_sent = lax.optimization_barrier((grad_other, weight_other))
        weight_crossed = swap_pair(weight_sent)
        grad_gated = project_back(out_grad, weight_mine) + project_back(grad_other, weight_other)
    else:
        grad_gated = project_back(
            lax.all_gather(out_grad, "ch", axis=1, tiled=True), out_weight
        )
    (grad_sent,) = by_blocks(grad_kernel, shape, [grad_gated, query_in], [message])
    grad_held = exchange(grad_sent)

    conv_held, spectrum = convolve(held.reshape(-1, tokens), tables, devices)
    if in_pairs:
        conv_held, weight_crossed = lax.optimization_barrier((conv_held, weight_crossed))
    conv_back = exchange(conv_held.reshape(message.shape))
    mixed_grad_held = convolve(grad_held.reshape(-1, tokens), tables, devices, spectrum)
    triple = jax.ShapeDtypeStruct((tokens, 3 * channels), BF16)
    gate_inputs = [conv_back, key_in, value_in, query_in, skip_row]
    if in_pairs:
        half = math.gcd(channels, WIDTH)
        gated = []
        for at in range(channels // half):
            block = jax.ShapeDtypeStruct((tokens, half), BF16)
            gated += by_blocks(gate_kernel, shape, gate_inputs, [block], only=at)
        crossed = [swap_pair(block) for block in gated]
        gated_out = jnp.concatenate(gated, axis=1)
    else:
        (gated_out,) = by_blocks(gate_kernel, shape, gate_inputs, [plain])
    mixed_grad_back = exchange(mixed_grad_held.reshape(message.shape))
    query_grad, near = by_blocks(
        query_grad_kernel, shape, gate_inputs + [grad_gated], [plain, triple], vmem_limit=LAST_LIMIT
    )
    if in_pairs:
        terms = jnp.dot(gated_out, weight_mine, preferred_element_type=F32)
        for at, block in enumerate(crossed[:-1]):
            rows = weight_crossed[at * half : (at + 1) * half, :]
            terms += jnp.dot(block, rows, preferred_element_type=F32)
        terms, query_grad, mixed_grad_back = lax.optimization_barrier(
            (terms, query_grad, mixed_grad_back)
        )
    key_grad, value_grad = by_blocks(
        input_grad_kernel,
        shape,
        [mixed_grad_back, near, skip_row, grad_gated],
        [plain, plain],
        vmem_limit=LAST_LIMIT,
    )
    if in_pairs:
        terms, key_grad, value_grad = lax.optimization_barrier((terms, key_grad, value_grad))
        mixed_out = project(terms, crossed[-1], weight_crossed, len(crossed) - 1, BF16)
    else:
        own_terms = jnp.dot(gated_out, out_weight, preferred_element_type=F32)
        mixed_out = lax.psum_scatter(own_terms, "ch", scatter_dimension=1, tiled=True)
    return (mixed_out.astype(BF16), query_grad, key_grad, value_grad)


def solution(mesh):
    spread = P("seq", "ch")
    placed = (spread, spread, spread, spread, P("ch"), P("ch", None), spread)
    return jax.shard_map(
        on_device, mesh=mesh, in_specs=placed, out_specs=(spread,) * 4, check_vma=False
    )
```

```python
import functools
import math

import jax
import jax.numpy as jnp
import ml_dtypes
import numpy as np
from jax import lax
from jax.experimental import pallas as pl
from jax.experimental.pallas import tpu as pltpu
from jax.sharding import PartitionSpec as P

F32 = jnp.float32
BF16 = jnp.bfloat16
LANES = 128


def split_table(table):
    high = table.astype(ml_dtypes.bfloat16)
    low = (table - high.astype(np.float64)).astype(ml_dtypes.bfloat16)
    return high, low


def transform_tables(devices, tokens_each):
    length = devices * tokens_each
    rows = length // LANES
    pieces = tokens_each // LANES
    row = np.arange(rows)
    n1 = (row % devices) * pieces + row // devices
    k1 = np.arange(rows)
    n2 = np.arange(LANES)

    def waves(turns, modulus):
        angle = (turns % modulus) * (2.0 * math.pi / modulus)
        return np.cos(angle), np.sin(angle)

    c, s = waves((4 * k1 + 1)[:, None] * n1[None, :], 4 * rows)
    high, low = split_table(np.concatenate([c, -s], axis=0))
    enter = np.concatenate([high, low], axis=1)
    high, low = split_table(np.concatenate([c.T, -s.T], axis=1) / length)
    leave = np.concatenate([high, low, high], axis=1)
    c, s = waves(n2[:, None] * n2[None, :], LANES)
    high, low = split_table(np.block([[c, -s], [s, c]]))
    forth = np.concatenate([high, low, high], axis=0)
    high, low = split_table(np.block([[c, s], [-s, c]]))
    back = np.concatenate([high, low, high], axis=0)
    c, s = waves((4 * k1 + 1)[:, None] * n2[None, :], 4 * length)
    turn = np.concatenate([c, s], axis=1).astype(np.float32)
    return enter, turn, np.concatenate([forth, back], axis=0), leave


def split_float(values):
    high = values.astype(BF16)
    return high, (values - high.astype(F32)).astype(BF16)


def mxu(left, right):
    return jnp.dot(left, right, preferred_element_type=F32)


def widen(held_ref, wide):
    for piece in range(wide.shape[0]):
        wide[piece] = held_ref[:, piece * LANES : (piece + 1) * LANES].astype(F32)


def narrow(wide, out_ref):
    for piece in range(wide.shape[0]):
        out_ref[:, piece * LANES : (piece + 1) * LANES] = wide[piece].astype(BF16)


def load_channels(wide, first, stride, devices, group):
    columns = []
    for member in range(group):
        place = pl.ds(first + member, devices, stride=stride)
        columns.append(
            jnp.concatenate([wide[piece, place, :] for piece in range(wide.shape[0])], axis=0)
        )
    return jnp.concatenate(columns, axis=1).astype(BF16)


def to_spectrum(data, group, enter_ref, turn_ref, waves_ref):
    rows = data.shape[0]
    entered = mxu(enter_ref[...], jnp.concatenate([data, data], axis=0))
    cosine, sine = turn_ref[:, :LANES], turn_ref[:, LANES:]
    turned = []
    for member in range(group):
        at = member * LANES
        real, imag = entered[:rows, at : at + LANES], entered[rows:, at : at + LANES]
        turned.append(
            jnp.concatenate([real * cosine + imag * sine, imag * cosine - real * sine], axis=1)
        )
    high, low = split_float(jnp.concatenate(turned, axis=0))
    return mxu(jnp.concatenate([high, high, low], axis=1), waves_ref[: 6 * LANES, :])


def from_spectrum(real, imag, group, turn_ref, waves_ref, leave_ref):
    high, low = split_float(jnp.concatenate([real, imag], axis=1))
    returned = mxu(jnp.concatenate([high, high, low], axis=1), waves_ref[6 * LANES :, :])
    rows = returned.shape[0] // group
    cosine, sine = turn_ref[:, :LANES], turn_ref[:, LANES:]
    turned = []
    for member in range(group):
        at = member * rows
        real, imag = returned[at : at + rows, :LANES], returned[at : at + rows, LANES:]
        turned.append(
            jnp.concatenate([real * cosine - imag * sine, real * sine + imag * cosine], axis=0)
        )
    high, low = split_float(jnp.concatenate(turned, axis=1))
    return mxu(leave_ref[...], jnp.concatenate([high, high, low], axis=0))


def store_channels(wide, first, stride, devices, group, result):
    for member in range(group):
        at = member * LANES
        place = pl.ds(first + member, devices, stride=stride)
        for piece in range(wide.shape[0]):
            row = piece * devices
            wide[piece, place, :] = result[row : row + devices, at : at + LANES]


def forward_kernel(
    devices,
    group,
    held_ref,
    enter_ref,
    turn_ref,
    waves_ref,
    leave_ref,
    out_ref,
    spectrum_ref,
    held_wide,
    out_wide,
):
    step = pl.program_id(0)
    channels = out_ref.shape[0] // devices

    @pl.when(step == 0)
    def _():
        widen(held_ref, held_wide)

    first = step * group
    data = load_channels(held_wide, first, 2 * channels, devices, group)
    taps = load_channels(held_wide, channels + first, 2 * channels, devices, group)
    into = (enter_ref, turn_ref, waves_ref)
    data = to_spectrum(data, group, *into)
    taps = to_spectrum(taps, group, *into)
    spectrum_ref[...] = taps
    data_real, data_imag = data[:, :LANES], data[:, LANES:]
    taps_real, taps_imag = taps[:, :LANES], taps[:, LANES:]
    result = from_spectrum(
        taps_real * data_real - taps_imag * data_imag,
        taps_real * data_imag + taps_imag * data_real,
        group,
        turn_ref,
        waves_ref,
        leave_ref,
    )
    store_channels(out_wide, first, channels, devices, group, result)

    @pl.when(step == pl.num_programs(0) - 1)
    def _():
        narrow(out_wide, out_ref)


def adjoint_kernel(
    devices,
    group,
    held_ref,
    enter_ref,
    turn_ref,
    waves_ref,
    leave_ref,
    spectrum_ref,
    out_ref,
    held_wide,
    out_wide,
):
    step = pl.program_id(0)
    channels = out_ref.shape[0] // devices

    @pl.when(step == 0)
    def _():
        widen(held_ref, held_wide)

    first = step * group
    data = load_channels(held_wide, first, channels, devices, group)
    data = to_spectrum(data, group, enter_ref, turn_ref, waves_ref)
    data_real, data_imag = data[:, :LANES], data[:, LANES:]
    taps_real, taps_imag = spectrum_ref[:, :LANES], spectrum_ref[:, LANES:]
    result = from_spectrum(
        taps_real * data_real + taps_imag * data_imag,
        taps_real * data_imag - taps_imag * data_real,
        group,
        turn_ref,
        waves_ref,
        leave_ref,
    )
    store_channels(out_wide, first, channels, devices, group, result)

    @pl.when(step == pl.num_programs(0) - 1)
    def _():
        narrow(out_wide, out_ref)


GROUP = 16
WIDTH = 512
VMEM_LIMIT = 60 * 1024 * 1024
LAST_LIMIT = 48 * 1024 * 1024


def whole_block(array):
    return pl.BlockSpec(array.shape, lambda i: (0,) * len(array.shape))


def convolve(held, tables, devices, spectrum=None):
    width, tokens = held.shape
    channels = width // devices // (2 if spectrum is None else 1)
    rows = devices * tokens // LANES
    group = math.gcd(GROUP, channels)
    out = jax.ShapeDtypeStruct((devices * channels, tokens), BF16)
    taps = jax.ShapeDtypeStruct((channels * rows, 2 * LANES), F32)
    taps_block = pl.BlockSpec((group * rows, 2 * LANES), lambda i: (i, 0))
    forward = spectrum is None
    transforms = 3 if forward else 2
    return pl.pallas_call(
        functools.partial(forward_kernel if forward else adjoint_kernel, devices, group),
        grid=(channels // group,),
        out_shape=(out, taps) if forward else out,
        in_specs=[whole_block(held)]
        + [whole_block(table) for table in tables]
        + ([] if forward else [taps_block]),
        out_specs=(whole_block(out), taps_block) if forward else whole_block(out),
        scratch_shapes=[
            pltpu.VMEM((tokens // LANES, width, LANES), F32),
            pltpu.VMEM((tokens // LANES, devices * channels, LANES), F32),
        ],
        compiler_params=pltpu.CompilerParams(vmem_limit_bytes=VMEM_LIMIT),
        cost_estimate=pl.CostEstimate(
            flops=transforms * 8 * 2 * 2 * LANES * 2 * LANES * rows * channels,
            bytes_accessed=8 * 1024 * 1024,
            transcendentals=0,
        ),
        name="convolve" if forward else "correlate",
    )(held, *tables, *([] if forward else [spectrum]))


def rows_of(block, which, channels):
    return block[which * channels : (which + 1) * channels, :]


def mix_kernel(key_ref, value_ref, taps_ref, message_ref):
    targets, both, _ = message_ref.shape
    channels = both // 2
    mixed = (key_ref[...].astype(F32) * value_ref[...].astype(F32)).astype(BF16).T
    taps = taps_ref[...].astype(BF16).T
    for target in range(targets):
        message_ref[target, :channels, :] = rows_of(mixed, target, channels)
        message_ref[target, channels:, :] = rows_of(taps, target, channels)


def grad_kernel(gated_ref, query_ref, message_ref):
    targets, channels, _ = message_ref.shape
    grad = (gated_ref[...] * query_ref[...].astype(F32)).astype(BF16).T
    for target in range(targets):
        message_ref[target] = rows_of(grad, target, channels)


def tokens_first(message_ref):
    targets, channels, tokens = message_ref.shape
    return message_ref[...].reshape(targets * channels, tokens).T.astype(F32)


def gate_kernel(message_ref, key_ref, value_ref, query_ref, skip_ref, gated_ref):
    mixed = key_ref[...].astype(F32) * value_ref[...].astype(F32)
    conv_out = tokens_first(message_ref) + skip_ref[...] * mixed
    gated_ref[...] = (query_ref[...].astype(F32) * conv_out).astype(BF16)


def query_grad_kernel(
    message_ref, key_ref, value_ref, query_ref, skip_ref, grad_ref, query_grad_ref, near_ref
):
    width = key_ref.shape[1]
    for at, ref in enumerate((key_ref, value_ref, query_ref)):
        near_ref[:, at * width : (at + 1) * width] = ref[...]
    mixed = key_ref[...].astype(F32) * value_ref[...].astype(F32)
    conv_out = tokens_first(message_ref) + skip_ref[...] * mixed
    query_grad_ref[...] = (grad_ref[...] * conv_out).astype(BF16)


def input_grad_kernel(
    message_ref, near_ref, skip_ref, grad_ref, key_grad_ref, value_grad_ref
):
    width = grad_ref.shape[1]
    key, value, query = (
        near_ref[:, at * width : (at + 1) * width].astype(F32) for at in range(3)
    )
    grad_mixed = tokens_first(message_ref) + skip_ref[...] * (grad_ref[...] * query)
    key_grad_ref[...] = (grad_mixed * value).astype(BF16)
    value_grad_ref[...] = (grad_mixed * key).astype(BF16)


def project_kernel(terms_ref, gated_ref, weight_ref, out_ref):
    total = terms_ref[...] + mxu(gated_ref[...], weight_ref[...])
    out_ref[...] = total.astype(out_ref.dtype)


def project(terms, gated, weight, at, kind):
    tokens, depth = gated.shape
    width = math.gcd(terms.shape[1], WIDTH)
    block = pl.BlockSpec((tokens, width), lambda j: (0, j))
    return pl.pallas_call(
        project_kernel,
        grid=(terms.shape[1] // width,),
        out_shape=jax.ShapeDtypeStruct(terms.shape, kind),
        in_specs=[
            block,
            pl.BlockSpec((tokens, depth), lambda j: (0, 0)),
            pl.BlockSpec((depth, width), lambda j: (at, j)),
        ],
        out_specs=block,
        cost_estimate=pl.CostEstimate(
            flops=2 * tokens * depth * terms.shape[1],
            bytes_accessed=6 * terms.size,
            transcendentals=0,
        ),
        compiler_params=pltpu.CompilerParams(vmem_limit_bytes=LAST_LIMIT),
        name="project",
    )(terms, gated, weight)


def by_blocks(kernel, shape, inputs, outs, only=None, vmem_limit=None):
    tokens, channels = shape
    steps = channels // math.gcd(channels, WIDTH)
    width = channels // steps

    def spec_of(array):
        def at(j):
            return j if only is None or array.shape[-1] == width else only

        if len(array.shape) == 3:
            targets, rows, _ = array.shape
            return pl.BlockSpec(
                (targets // steps, rows, tokens), lambda j: (j if only is None else only, 0, 0)
            )
        size = width if only is not None else array.shape[1] // steps
        return pl.BlockSpec((array.shape[0], size), lambda j: (0, at(j)))

    moved = sum(a.size * a.dtype.itemsize for a in list(inputs) + list(outs))
    return pl.pallas_call(
        kernel,
        grid=(steps if only is None else 1,),
        out_shape=outs,
        in_specs=[spec_of(a) for a in inputs],
        out_specs=[spec_of(a) for a in outs],
        cost_estimate=pl.CostEstimate(
            flops=4 * tokens * channels, bytes_accessed=moved, transcendentals=0
        ),
        compiler_params=pltpu.CompilerParams(vmem_limit_bytes=vmem_limit or VMEM_LIMIT),
    )(*inputs)


def exchange(values):
    return lax.all_to_all(values, "seq", split_axis=0, concat_axis=0, tiled=True)


def swap_pair(values):
    return lax.ppermute(values, "ch", [(0, 1), (1, 0)])


def on_device(query_in, key_in, value_in, filter_taps, skip_gain, out_weight, out_grad):
    devices = lax.axis_size("seq")
    in_pairs = lax.axis_size("ch") == 2
    shape = key_in.shape
    tokens, channels = shape
    each = channels // devices
    tables = [jnp.asarray(table) for table in transform_tables(devices, tokens)]
    skip_row = skip_gain.reshape(1, channels)
    plain = jax.ShapeDtypeStruct(shape, BF16)
    message = jax.ShapeDtypeStruct((devices, each, tokens), BF16)
    double = jax.ShapeDtypeStruct((devices, 2 * each, tokens), BF16)
    over_columns = (((1,), (1,)), ((), ()))

    def project_back(grad, weight):
        return lax.dot_general(grad, weight, over_columns, preferred_element_type=F32)

    if in_pairs:
        grad_other = swap_pair(out_grad)
    (sent,) = by_blocks(mix_kernel, shape, [key_in, value_in, filter_taps], [double])
    held = exchange(sent)

    if in_pairs:
        mine = lax.axis_index("ch") * channels
        other = channels - mine
        weight_mine = lax.dynamic_slice_in_dim(out_weight, mine, channels, axis=1)
        weight_other = lax.dynamic_slice_in_dim(out_weight, other, channels, axis=1)
        grad_other, weight_sent = lax.optimization_barrier((grad_other, weight_other))
        weight_crossed = swap_pair(weight_sent)
        grad_gated = project_back(out_grad, weight_mine) + project_back(grad_other, weight_other)
    else:
        grad_gated = project_back(
            lax.all_gather(out_grad, "ch", axis=1, tiled=True), out_weight
        )
    (grad_sent,) = by_blocks(grad_kernel, shape, [grad_gated, query_in], [message])
    grad_held = exchange(grad_sent)

    conv_held, spectrum = convolve(held.reshape(-1, tokens), tables, devices)
    if in_pairs:
        conv_held, weight_crossed = lax.optimization_barrier((conv_held, weight_crossed))
    conv_back = exchange(conv_held.reshape(message.shape))
    mixed_grad_held = convolve(grad_held.reshape(-1, tokens), tables, devices, spectrum)
    triple = jax.ShapeDtypeStruct((tokens, 3 * channels), BF16)
    gate_inputs = [conv_back, key_in, value_in, query_in, skip_row]
    if in_pairs:
        half = math.gcd(channels, WIDTH)
        gated = []
        for at in range(channels // half):
            block = jax.ShapeDtypeStruct((tokens, half), BF16)
            gated += by_blocks(gate_kernel, shape, gate_inputs, [block], only=at)
        crossed = [swap_pair(block) for block in gated]
        gated_out = jnp.concatenate(gated, axis=1)
    else:
        (gated_out,) = by_blocks(gate_kernel, shape, gate_inputs, [plain])
    mixed_grad_back = exchange(mixed_grad_held.reshape(message.shape))
    query_grad, near = by_blocks(
        query_grad_kernel, shape, gate_inputs + [grad_gated], [plain, triple], vmem_limit=LAST_LIMIT
    )
    if in_pairs:
        terms = jnp.dot(gated_out, weight_mine, preferred_element_type=F32)
        for at, block in enumerate(crossed[:-1]):
            rows = weight_crossed[at * half : (at + 1) * half, :]
            terms += jnp.dot(block, rows, preferred_element_type=F32)
        terms, query_grad, mixed_grad_back = lax.optimization_barrier(
            (terms, query_grad, mixed_grad_back)
        )
    key_grad, value_grad = by_blocks(
        input_grad_kernel,
        shape,
        [mixed_grad_back, near, skip_row, grad_gated],
        [plain, plain],
        vmem_limit=LAST_LIMIT,
    )
    if in_pairs:
        terms, key_grad, value_grad = lax.optimization_barrier((terms, key_grad, value_grad))
        mixed_out = project(terms, crossed[-1], weight_crossed, len(crossed) - 1, BF16)
    else:
        own_terms = jnp.dot(gated_out, out_weight, preferred_element_type=F32)
        mixed_out = lax.psum_scatter(own_terms, "ch", scatter_dimension=1, tiled=True)
    return (mixed_out.astype(BF16), query_grad, key_grad, value_grad)


def solution(mesh):
    spread = P("seq", "ch")
    placed = (spread, spread, spread, spread, P("ch"), P("ch", None), spread)
    return jax.shard_map(
        on_device, mesh=mesh, in_specs=placed, out_specs=(spread,) * 4, check_vma=False
    )
```

```python
import functools
import math

import jax
import jax.numpy as jnp
import ml_dtypes
import numpy as np
from jax import lax
from jax.experimental import pallas as pl
from jax.experimental.pallas import tpu as pltpu
from jax.sharding import PartitionSpec as P

F32 = jnp.float32
BF16 = jnp.bfloat16
LANES = 128


def split_table(table):
    high = table.astype(ml_dtypes.bfloat16)
    low = (table - high.astype(np.float64)).astype(ml_dtypes.bfloat16)
    return high, low


def transform_tables(devices, tokens_each):
    length = devices * tokens_each
    rows = length // LANES
    pieces = tokens_each // LANES
    row = np.arange(rows)
    n1 = (row % devices) * pieces + row // devices
    k1 = np.arange(rows)
    n2 = np.arange(LANES)

    def waves(turns, modulus):
        angle = (turns % modulus) * (2.0 * math.pi / modulus)
        return np.cos(angle), np.sin(angle)

    c, s = waves((4 * k1 + 1)[:, None] * n1[None, :], 4 * rows)
    high, low = split_table(np.concatenate([c, -s], axis=0))
    enter = np.concatenate([high, low], axis=1)
    high, low = split_table(np.concatenate([c.T, -s.T], axis=1) / length)
    leave = np.concatenate([high, low, high], axis=1)
    c, s = waves(n2[:, None] * n2[None, :], LANES)
    high, low = split_table(np.block([[c, -s], [s, c]]))
    forth = np.concatenate([high, low, high], axis=0)
    high, low = split_table(np.block([[c, s], [-s, c]]))
    back = np.concatenate([high, low, high], axis=0)
    c, s = waves((4 * k1 + 1)[:, None] * n2[None, :], 4 * length)
    turn = np.concatenate([c, s], axis=1).astype(np.float32)
    return enter, turn, np.concatenate([forth, back], axis=0), leave


def split_float(values):
    high = values.astype(BF16)
    return high, (values - high.astype(F32)).astype(BF16)


def mxu(left, right):
    return jnp.dot(left, right, preferred_element_type=F32)


def widen(held_ref, wide):
    for piece in range(wide.shape[0]):
        block = held_ref[:, piece * LANES : (piece + 1) * LANES].astype(F32)
        wide[piece, : block.shape[0], :] = block


def narrow(wide, out_ref):
    for piece in range(wide.shape[0]):
        block = wide[piece, : out_ref.shape[0], :]
        out_ref[:, piece * LANES : (piece + 1) * LANES] = block.astype(BF16)


def load_channels(wide, first, stride, devices, group):
    columns = []
    for member in range(group):
        place = pl.ds(first + member, devices, stride=stride)
        columns.append(
            jnp.concatenate([wide[piece, place, :] for piece in range(wide.shape[0])], axis=0)
        )
    return jnp.concatenate(columns, axis=1).astype(BF16)


def to_spectrum(data, group, enter_ref, turn_ref, waves_ref):
    rows = data.shape[0]
    entered = mxu(enter_ref[...], jnp.concatenate([data, data], axis=0))
    cosine, sine = turn_ref[:, :LANES], turn_ref[:, LANES:]
    turned = []
    for member in range(group):
        at = member * LANES
        real, imag = entered[:rows, at : at + LANES], entered[rows:, at : at + LANES]
        turned.append(
            jnp.concatenate([real * cosine + imag * sine, imag * cosine - real * sine], axis=1)
        )
    high, low = split_float(jnp.concatenate(turned, axis=0))
    return mxu(jnp.concatenate([high, high, low], axis=1), waves_ref[: 6 * LANES, :])


def from_spectrum(real, imag, group, turn_ref, waves_ref, leave_ref):
    high, low = split_float(jnp.concatenate([real, imag], axis=1))
    returned = mxu(jnp.concatenate([high, high, low], axis=1), waves_ref[6 * LANES :, :])
    rows = returned.shape[0] // group
    cosine, sine = turn_ref[:, :LANES], turn_ref[:, LANES:]
    turned = []
    for member in range(group):
        at = member * rows
        real, imag = returned[at : at + rows, :LANES], returned[at : at + rows, LANES:]
        turned.append(
            jnp.concatenate([real * cosine - imag * sine, real * sine + imag * cosine], axis=0)
        )
    high, low = split_float(jnp.concatenate(turned, axis=1))
    return mxu(leave_ref[...], jnp.concatenate([high, high, low], axis=0))


def store_channels(wide, first, stride, devices, group, result):
    for member in range(group):
        at = member * LANES
        place = pl.ds(first + member, devices, stride=stride)
        for piece in range(wide.shape[0]):
            row = piece * devices
            wide[piece, place, :] = result[row : row + devices, at : at + LANES]


def forward_kernel(
    devices,
    group,
    held_ref,
    enter_ref,
    turn_ref,
    waves_ref,
    leave_ref,
    out_ref,
    spectrum_ref,
    held_wide,
    out_wide,
):
    step = pl.program_id(0)
    channels = out_ref.shape[0] // devices

    @pl.when(step == 0)
    def _():
        widen(held_ref, held_wide)

    first = step * group
    data = load_channels(held_wide, first, 2 * channels, devices, group)
    taps = load_channels(held_wide, channels + first, 2 * channels, devices, group)
    into = (enter_ref, turn_ref, waves_ref)
    data = to_spectrum(data, group, *into)
    taps = to_spectrum(taps, group, *into)
    spectrum_ref[...] = taps
    data_real, data_imag = data[:, :LANES], data[:, LANES:]
    taps_real, taps_imag = taps[:, :LANES], taps[:, LANES:]
    result = from_spectrum(
        taps_real * data_real - taps_imag * data_imag,
        taps_real * data_imag + taps_imag * data_real,
        group,
        turn_ref,
        waves_ref,
        leave_ref,
    )
    store_channels(out_wide, first, channels, devices, group, result)

    @pl.when(step == pl.num_programs(0) - 1)
    def _():
        narrow(out_wide, out_ref)


def adjoint_kernel(
    devices,
    group,
    held_ref,
    enter_ref,
    turn_ref,
    waves_ref,
    leave_ref,
    spectrum_ref,
    out_ref,
    held_wide,
    out_wide,
):
    step = pl.program_id(0)
    channels = out_ref.shape[0] // devices

    @pl.when(step == 0)
    def _():
        widen(held_ref, held_wide)

    first = step * group
    data = load_channels(held_wide, first, channels, devices, group)
    data = to_spectrum(data, group, enter_ref, turn_ref, waves_ref)
    data_real, data_imag = data[:, :LANES], data[:, LANES:]
    taps_real, taps_imag = spectrum_ref[:, :LANES], spectrum_ref[:, LANES:]
    result = from_spectrum(
        taps_real * data_real + taps_imag * data_imag,
        taps_real * data_imag - taps_imag * data_real,
        group,
        turn_ref,
        waves_ref,
        leave_ref,
    )
    store_channels(out_wide, first, channels, devices, group, result)

    @pl.when(step == pl.num_programs(0) - 1)
    def _():
        narrow(out_wide, out_ref)


GROUP = 16
WIDTH = 512
VMEM_LIMIT = 60 * 1024 * 1024
LAST_LIMIT = 48 * 1024 * 1024


def whole_block(array):
    return pl.BlockSpec(array.shape, lambda i: (0,) * len(array.shape))


def convolve(held, tables, devices, spectrum=None):
    width, tokens = held.shape
    channels = width // devices // (2 if spectrum is None else 1)
    rows = devices * tokens // LANES
    group = math.gcd(GROUP, channels)
    out = jax.ShapeDtypeStruct((devices * channels, tokens), BF16)
    taps = jax.ShapeDtypeStruct((channels * rows, 2 * LANES), F32)
    taps_block = pl.BlockSpec((group * rows, 2 * LANES), lambda i: (i, 0))
    forward = spectrum is None
    transforms = 3 if forward else 2
    return pl.pallas_call(
        functools.partial(forward_kernel if forward else adjoint_kernel, devices, group),
        grid=(channels // group,),
        out_shape=(out, taps) if forward else out,
        in_specs=[whole_block(held)]
        + [whole_block(table) for table in tables]
        + ([] if forward else [taps_block]),
        out_specs=(whole_block(out), taps_block) if forward else whole_block(out),
        scratch_shapes=[
            pltpu.VMEM((tokens // LANES, width + width // devices, LANES), F32),
            pltpu.VMEM((tokens // LANES, (devices + 1) * channels, LANES), F32),
        ],
        compiler_params=pltpu.CompilerParams(vmem_limit_bytes=VMEM_LIMIT),
        cost_estimate=pl.CostEstimate(
            flops=transforms * 8 * 2 * 2 * LANES * 2 * LANES * rows * channels,
            bytes_accessed=8 * 1024 * 1024,
            transcendentals=0,
        ),
        name="convolve" if forward else "correlate",
    )(held, *tables, *([] if forward else [spectrum]))


def rows_of(block, which, channels):
    return block[which * channels : (which + 1) * channels, :]


def mix_kernel(key_ref, value_ref, taps_ref, message_ref):
    targets, both, _ = message_ref.shape
    channels = both // 2
    mixed = (key_ref[...].astype(F32) * value_ref[...].astype(F32)).astype(BF16).T
    taps = taps_ref[...].astype(BF16).T
    for target in range(targets):
        message_ref[target, :channels, :] = rows_of(mixed, target, channels)
        message_ref[target, channels:, :] = rows_of(taps, target, channels)


def grad_kernel(gated_ref, query_ref, message_ref):
    targets, channels, _ = message_ref.shape
    grad = (gated_ref[...] * query_ref[...].astype(F32)).astype(BF16).T
    for target in range(targets):
        message_ref[target] = rows_of(grad, target, channels)


def tokens_first(message_ref):
    targets, channels, tokens = message_ref.shape
    return message_ref[...].reshape(targets * channels, tokens).T.astype(F32)


def gate_kernel(message_ref, key_ref, value_ref, query_ref, skip_ref, gated_ref):
    mixed = key_ref[...].astype(F32) * value_ref[...].astype(F32)
    conv_out = tokens_first(message_ref) + skip_ref[...] * mixed
    gated_ref[...] = (query_ref[...].astype(F32) * conv_out).astype(BF16)


def query_grad_kernel(
    message_ref, key_ref, value_ref, query_ref, skip_ref, grad_ref, query_grad_ref, near_ref
):
    width = key_ref.shape[1]
    for at, ref in enumerate((key_ref, value_ref, query_ref)):
        near_ref[:, at * width : (at + 1) * width] = ref[...]
    mixed = key_ref[...].astype(F32) * value_ref[...].astype(F32)
    conv_out = tokens_first(message_ref) + skip_ref[...] * mixed
    query_grad_ref[...] = (grad_ref[...] * conv_out).astype(BF16)


def input_grad_kernel(
    message_ref, near_ref, skip_ref, grad_ref, key_grad_ref, value_grad_ref
):
    width = grad_ref.shape[1]
    key, value, query = (
        near_ref[:, at * width : (at + 1) * width].astype(F32) for at in range(3)
    )
    grad_mixed = tokens_first(message_ref) + skip_ref[...] * (grad_ref[...] * query)
    key_grad_ref[...] = (grad_mixed * value).astype(BF16)
    value_grad_ref[...] = (grad_mixed * key).astype(BF16)


def project_kernel(terms_ref, gated_ref, weight_ref, out_ref):
    total = terms_ref[...] + mxu(gated_ref[...], weight_ref[...])
    out_ref[...] = total.astype(out_ref.dtype)


def project(terms, gated, weight, at, kind):
    tokens, depth = gated.shape
    width = math.gcd(terms.shape[1], WIDTH)
    block = pl.BlockSpec((tokens, width), lambda j: (0, j))
    return pl.pallas_call(
        project_kernel,
        grid=(terms.shape[1] // width,),
        out_shape=jax.ShapeDtypeStruct(terms.shape, kind),
        in_specs=[
            block,
            pl.BlockSpec((tokens, depth), lambda j: (0, 0)),
            pl.BlockSpec((depth, width), lambda j: (at, j)),
        ],
        out_specs=block,
        cost_estimate=pl.CostEstimate(
            flops=2 * tokens * depth * terms.shape[1],
            bytes_accessed=6 * terms.size,
            transcendentals=0,
        ),
        compiler_params=pltpu.CompilerParams(vmem_limit_bytes=LAST_LIMIT),
        name="project",
    )(terms, gated, weight)


def by_blocks(kernel, shape, inputs, outs, only=None, vmem_limit=None):
    tokens, channels = shape
    steps = channels // math.gcd(channels, WIDTH)
    width = channels // steps

    def spec_of(array):
        def at(j):
            return j if only is None or array.shape[-1] == width else only

        if len(array.shape) == 3:
            targets, rows, _ = array.shape
            return pl.BlockSpec(
                (targets // steps, rows, tokens), lambda j: (j if only is None else only, 0, 0)
            )
        size = width if only is not None else array.shape[1] // steps
        return pl.BlockSpec((array.shape[0], size), lambda j: (0, at(j)))

    moved = sum(a.size * a.dtype.itemsize for a in list(inputs) + list(outs))
    return pl.pallas_call(
        kernel,
        grid=(steps if only is None else 1,),
        out_shape=outs,
        in_specs=[spec_of(a) for a in inputs],
        out_specs=[spec_of(a) for a in outs],
        cost_estimate=pl.CostEstimate(
            flops=4 * tokens * channels, bytes_accessed=moved, transcendentals=0
        ),
        compiler_params=pltpu.CompilerParams(vmem_limit_bytes=vmem_limit or VMEM_LIMIT),
    )(*inputs)


def exchange(values):
    return lax.all_to_all(values, "seq", split_axis=0, concat_axis=0, tiled=True)


def swap_pair(values):
    return lax.ppermute(values, "ch", [(0, 1), (1, 0)])


def on_device(query_in, key_in, value_in, filter_taps, skip_gain, out_weight, out_grad):
    devices = lax.axis_size("seq")
    in_pairs = lax.axis_size("ch") == 2
    shape = key_in.shape
    tokens, channels = shape
    each = channels // devices
    tables = [jnp.asarray(table) for table in transform_tables(devices, tokens)]
    skip_row = skip_gain.reshape(1, channels)
    plain = jax.ShapeDtypeStruct(shape, BF16)
    message = jax.ShapeDtypeStruct((devices, each, tokens), BF16)
    double = jax.ShapeDtypeStruct((devices, 2 * each, tokens), BF16)
    over_columns = (((1,), (1,)), ((), ()))

    def project_back(grad, weight):
        return lax.dot_general(grad, weight, over_columns, preferred_element_type=F32)

    if in_pairs:
        grad_other = swap_pair(out_grad)
    (sent,) = by_blocks(mix_kernel, shape, [key_in, value_in, filter_taps], [double])
    held = exchange(sent)

    if in_pairs:
        mine = lax.axis_index("ch") * channels
        other = channels - mine
        weight_mine = lax.dynamic_slice_in_dim(out_weight, mine, channels, axis=1)
        weight_other = lax.dynamic_slice_in_dim(out_weight, other, channels, axis=1)
        grad_other, weight_sent = lax.optimization_barrier((grad_other, weight_other))
        weight_crossed = swap_pair(weight_sent)
        grad_gated = project_back(out_grad, weight_mine) + project_back(grad_other, weight_other)
    else:
        grad_gated = project_back(
            lax.all_gather(out_grad, "ch", axis=1, tiled=True), out_weight
        )
    (grad_sent,) = by_blocks(grad_kernel, shape, [grad_gated, query_in], [message])
    grad_held = exchange(grad_sent)

    conv_held, spectrum = convolve(held.reshape(-1, tokens), tables, devices)
    if in_pairs:
        conv_held, weight_crossed = lax.optimization_barrier((conv_held, weight_crossed))
    conv_back = exchange(conv_held.reshape(message.shape))
    mixed_grad_held = convolve(grad_held.reshape(-1, tokens), tables, devices, spectrum)
    triple = jax.ShapeDtypeStruct((tokens, 3 * channels), BF16)
    gate_inputs = [conv_back, key_in, value_in, query_in, skip_row]
    if in_pairs:
        half = math.gcd(channels, WIDTH)
        gated = []
        for at in range(channels // half):
            block = jax.ShapeDtypeStruct((tokens, half), BF16)
            gated += by_blocks(gate_kernel, shape, gate_inputs, [block], only=at)
        crossed = [swap_pair(block) for block in gated]
        gated_out = jnp.concatenate(gated, axis=1)
    else:
        (gated_out,) = by_blocks(gate_kernel, shape, gate_inputs, [plain])
    mixed_grad_back = exchange(mixed_grad_held.reshape(message.shape))
    query_grad, near = by_blocks(
        query_grad_kernel, shape, gate_inputs + [grad_gated], [plain, triple], vmem_limit=LAST_LIMIT
    )
    if in_pairs:
        terms = jnp.dot(gated_out, weight_mine, preferred_element_type=F32)
        for at, block in enumerate(crossed[:-1]):
            rows = weight_crossed[at * half : (at + 1) * half, :]
            terms += jnp.dot(block, rows, preferred_element_type=F32)
        terms, query_grad, mixed_grad_back = lax.optimization_barrier(
            (terms, query_grad, mixed_grad_back)
        )
    key_grad, value_grad = by_blocks(
        input_grad_kernel,
        shape,
        [mixed_grad_back, near, skip_row, grad_gated],
        [plain, plain],
        vmem_limit=LAST_LIMIT,
    )
    if in_pairs:
        terms, key_grad, value_grad = lax.optimization_barrier((terms, key_grad, value_grad))
        mixed_out = project(terms, crossed[-1], weight_crossed, len(crossed) - 1, BF16)
    else:
        own_terms = jnp.dot(gated_out, out_weight, preferred_element_type=F32)
        mixed_out = lax.psum_scatter(own_terms, "ch", scatter_dimension=1, tiled=True)
    return (mixed_out.astype(BF16), query_grad, key_grad, value_grad)


def solution(mesh):
    spread = P("seq", "ch")
    placed = (spread, spread, spread, spread, P("ch"), P("ch", None), spread)
    return jax.shard_map(
        on_device, mesh=mesh, in_specs=placed, out_specs=(spread,) * 4, check_vma=False
    )
```
